128 devices in a mesh: ty: 16 (over z, x_lo, core), tx: 8 (over x_hi, y).
Axes of the slice: x: 4 (x_hi: 2, x_lo: 2; x = x_hi * 2 + x_lo), y: 4, z: 4, core: 2. Of those that a mesh axis runs over, the one named last changes fastest.
Arguments:
- image: float32 [4096, 4096], P('ty', 'tx'), may hold values from -6 to 6
- noise: float32 [2, 4096, 4096], P(None, 'ty', 'tx'), may hold values from -6 to 6
- offsets: int32 [2, 2], replicated, may hold values from 1 to 7, as said below
- key_mask: int32 [256, 256], P('ty', 'tx'), may hold values 0 or 1
- gains: float32 [2, 4096, 4096], P(None, ('ty', 'tx')), may hold values from -1 to 1
- observed: float32 [2, 4096, 4096], P(None, ('ty', 'tx')), may hold values from -6 to 6
- vis_weight: float32 [4096, 4096], P(('ty', 'tx')), may hold values from 0.05 to 1
- w_embed: bfloat16 [256, 512], replicated, may hold values from -0.375 to 0.375
- w_qkv: bfloat16 [2, 512, 1536], replicated, as said below
- w_proj: bfloat16 [2, 512, 512], replicated, may hold values from -0.25 to 0.25
- w_up: bfloat16 [2, 512, 2048], replicated, may hold values from -0.25 to 0.25
- w_down: bfloat16 [2, 2048, 512], replicated, may hold values from -0.125 to 0.125
- w_unembed: bfloat16 [512, 256], replicated, may hold values from -0.25 to 0.25
- norm_gains: float32 [2, 2, 512], replicated, may hold values from 0.1 to 1.9
Outputs:
- sampled: float32 [4096, 4096], P('ty', 'tx')
The draws below stay inside these ranges and needn't reach their ends.
Inputs may be any that keep to these rules, and one draw needn't show every extreme that they name: `offsets`: each entry lies in 1 to 7, and some entry equals 7. `w_qkv`: columns ordered by query, key or value, then head, then feature of the head.
All inputs are finite; a program needn't handle non-finite values. No bound on the sum of `key_mask` on one device may be relied on, other than what follows from the above.
Results may differ from the reference program's by a relative error of at most 0.04.
Values may be sent and summed in bfloat16 or wider, within the bound.
A program may use at most 128 MiB of HBM per device.

```python
import math
import jax
import jax.numpy as jnp
from jax import lax

N = 4096
PATCH = 16
WIN = 8
D = 512
HEADS = 8
FF = 2048
STEPS = 2
BLOCKS = 2
TOK = 256
PIXELS = 256


def draw_offsets(key, part):
    key = jax.random.fold_in(key, 5)
    drawn = jax.random.randint(key, (STEPS * 2,), 1, WIN)
    chosen = jax.random.randint(jax.random.fold_in(key, 1), (), 0, STEPS * 2)
    flat = jnp.where(jnp.arange(STEPS * 2) == chosen, WIN - 1, drawn)
    return flat.reshape(STEPS, 2).astype(jnp.int32)


def draw_w_qkv(key, part):
    key = jax.random.fold_in(key, 11)
    base = jax.random.normal(key, (BLOCKS, D, 3, HEADS, D // HEADS), jnp.float32) * D ** (-0.5)
    return base.reshape(BLOCKS, D, 3 * D).astype(jnp.bfloat16)


def touch_ends(values, rng, smallest, high):
    longest = values.shape.index(max(values.shape))
    spots = []
    for shift in (0, 1):
        where = [jax.random.randint(jax.random.fold_in(rng, axis), (), 0, length) for axis, length in enumerate(values.shape)]
        where[longest] = (where[longest] + shift) % values.shape[longest]
        spots.append(tuple(where))
    return values.at[spots[0]].set(smallest).at[spots[1]].set(high)


def level_of(stream_key, dims, cuts, smallest, top_value):
    factor_of, own = 1.0, jax.random.fold_in(stream_key, 6)
    for dim, shards_of in cuts:
        heights = jnp.exp(jax.random.uniform(jax.random.fold_in(own, dim), (shards_of,), jnp.float32, smallest / len(cuts), top_value / len(cuts)))
        factor_of = factor_of * jnp.repeat(heights, dims[dim] // shards_of).reshape([-1 if axis == dim else 1 for axis in range(len(dims))])
    return factor_of


def gaussian(own_key, shape, scale, limit, cuts=(), kind=jnp.bfloat16):
    entries = jax.random.normal(own_key, shape, jnp.float32) * scale
    if len(cuts) > 0:
        entries = level_of(own_key, shape, cuts, -0.22, 0.18) * entries
    return jnp.clip(entries, min=-limit, max=limit).astype(kind)


def setup_inputs(seed: int = 0) -> dict:
    arg_keys = jax.random.split(jax.random.key(seed), 15)
    image = gaussian(arg_keys[0], (N, N), 1.0, 6.0, ((0, 16), (1, 8)), jnp.float32)
    noise = gaussian(arg_keys[1], (STEPS, N, N), 1.0, 6.0, ((1, 16), (2, 8)), jnp.float32)
    offsets = draw_offsets(jax.random.fold_in(arg_keys[14], 71), 0)
    key_mask = touch_ends((jax.random.randint(arg_keys[3], (TOK, TOK), 0, 8) < 7).astype(jnp.int32), jax.random.fold_in(arg_keys[3], 1), 0, 1)
    gains = jnp.clip(jax.random.uniform(arg_keys[4], (2, N, N), jnp.float32, -1.0, 1.0) * level_of(arg_keys[4], (2, N, N), ((1, 128),), -0.4, 0.0), -1.0, 1.0)
    observed = gaussian(arg_keys[5], (2, N, N), 1.0, 6.0, ((1, 128),), jnp.float32)
    vis_weight = jnp.clip(jnp.exp(math.log(1.0) - 2.9957323 * jax.random.uniform(arg_keys[6], (N, N), jnp.float32) ** level_of(arg_keys[6], (N, N), ((0, 128),), -0.2, 0.2)), 0.05, 1.0)
    w_embed = gaussian(arg_keys[7], (PIXELS, D), PIXELS ** -0.5, 0.375)
    w_qkv = draw_w_qkv(jax.random.fold_in(arg_keys[14], 71), 0)
    w_proj = gaussian(arg_keys[9], (BLOCKS, D, D), D ** -0.5, 0.25)
    w_up = gaussian(arg_keys[10], (BLOCKS, D, FF), D ** -0.5, 0.25)
    w_down = gaussian(arg_keys[11], (BLOCKS, FF, D), FF ** -0.5, 0.125)
    w_unembed = gaussian(arg_keys[12], (D, PIXELS), D ** -0.5, 0.25)
    norm_gains = jnp.clip(1.0 + 0.18 * jax.random.normal(arg_keys[13], (BLOCKS, 2, D), jnp.float32), 0.1, 1.9)
    return {"image": image, "noise": noise, "offsets": offsets, "key_mask": key_mask, "gains": gains, "observed": observed, "vis_weight": vis_weight, "w_embed": w_embed, "w_qkv": w_qkv, "w_proj": w_proj, "w_up": w_up, "w_down": w_down, "w_unembed": w_unembed, "norm_gains": norm_gains}


SIGMAS = (0.8, 0.5, 0.3)
STEP_SIZES = (0.9, 0.7)
EPSILON = 1e-05

def layer_norm(values, gain):
    centre = lax.optimization_barrier(jnp.mean(values, axis=-1, keepdims=True))
    shifted = values - centre
    spread = lax.optimization_barrier(jnp.mean(shifted * shifted, axis=-1, keepdims=True))
    return shifted * lax.rsqrt(spread + EPSILON) * gain

def to_windows(grid):
    rows, cols, feats = grid.shape
    shaped = grid.reshape(rows // WIN, WIN, cols // WIN, WIN, feats).transpose(0, 2, 1, 3, 4)
    return shaped.reshape(rows // WIN * (cols // WIN), WIN * WIN, feats)

def from_windows(windows, rows, cols):
    feats = windows.shape[-1]
    shaped = windows.reshape(rows // WIN, cols // WIN, WIN, WIN, feats).transpose(0, 2, 1, 3, 4)
    return shaped.reshape(rows, cols, feats)

def attention(normed, labels, keep, w_qkv, w_proj):
    rows, cols = (normed.shape[0], normed.shape[1])
    mixed = jnp.dot(normed.reshape(rows * cols, D), w_qkv, preferred_element_type=jnp.float32)
    mixed = to_windows(mixed.astype(jnp.bfloat16).reshape(rows, cols, 3 * D))
    number = mixed.shape[0]
    parts = mixed.reshape(number, WIN * WIN, 3, HEADS, D // HEADS).astype(jnp.float32)
    scores = jnp.einsum('wqhe,wkhe->whqk', parts[:, :, 0], parts[:, :, 1]) / math.sqrt(D // HEADS)
    label_win = to_windows(labels[:, :, None])[:, :, 0]
    keep_win = to_windows(keep[:, :, None])[:, :, 0]
    same = label_win[:, :, None] == label_win[:, None, :]
    visible = (keep_win[:, None, :] == 1) | jnp.eye(WIN * WIN, dtype=bool)[None]
    allowed = (same & visible)[:, None]
    scores = jnp.where(allowed, scores, -1e+30)
    largest = lax.optimization_barrier(jnp.max(scores, axis=-1, keepdims=True))
    weights = jnp.exp(scores - largest)
    probs = (weights / lax.optimization_barrier(jnp.sum(weights, axis=-1, keepdims=True))).astype(jnp.bfloat16)
    attended = jnp.einsum('whqk,wkhe->wqhe', probs.astype(jnp.float32), parts[:, :, 2]).astype(jnp.bfloat16)
    attended = from_windows(attended.reshape(number, WIN * WIN, D), rows, cols)
    projected = jnp.dot(attended.reshape(rows * cols, D), w_proj, preferred_element_type=jnp.float32)
    return projected.reshape(rows, cols, D)

def swin_block(grid, labels, keep, w_qkv, w_proj, w_up, w_down, gains):
    rows, cols = (grid.shape[0], grid.shape[1])
    flow = grid.astype(jnp.float32)
    normed = layer_norm(flow, gains[0]).astype(jnp.bfloat16)
    flow = flow + attention(normed, labels, keep, w_qkv, w_proj)
    normed = layer_norm(flow, gains[1]).astype(jnp.bfloat16).reshape(rows * cols, D)
    hidden = jax.nn.gelu(jnp.dot(normed, w_up, preferred_element_type=jnp.float32), approximate=True)
    hidden = hidden.astype(jnp.bfloat16)
    flow = flow + jnp.dot(hidden, w_down, preferred_element_type=jnp.float32).reshape(rows, cols, D)
    return flow.astype(jnp.bfloat16)

def banded(grid, labels, keep, w_qkv, w_proj, w_up, w_down, gains):
    side = grid.shape[0]
    bands = side // WIN

    def one_band(band):
        return swin_block(band[0], band[1], band[2], w_qkv, w_proj, w_up, w_down, gains)
    stacked = lax.map(one_band, (grid.reshape(bands, WIN, side, D), labels.reshape(bands, WIN, side), keep.reshape(bands, WIN, side)))
    return stacked.reshape(side, side, D)

def patches_of(picture):
    rows, cols = picture.shape
    shaped = picture.reshape(rows // PATCH, PATCH, cols // PATCH, PATCH).transpose(0, 2, 1, 3)
    return shaped.reshape(rows // PATCH, cols // PATCH, PATCH * PATCH).astype(jnp.bfloat16)

def image_of(pieces):
    rows, cols = (pieces.shape[0], pieces.shape[1])
    shaped = pieces.reshape(rows, cols, PATCH, PATCH).transpose(0, 2, 1, 3)
    return shaped.reshape(rows * PATCH, cols * PATCH)

def region(index, shift):
    side = N // PATCH
    return jnp.where(index < side - WIN, 0, jnp.where(index < side - shift, 1, 2)).astype(jnp.int32)

def likelihood(state, gains, observed, vis_weight):
    spectrum = jnp.fft.fft2(state).T / N
    gain = lax.complex(gains[0], gains[1])
    seen = lax.complex(observed[0], observed[1])
    back = jnp.conj(gain) * (vis_weight * (gain * spectrum - seen))
    return jnp.real(jnp.fft.ifft2(back.T)) * N

def reference(image, noise, offsets, key_mask, gains, observed, vis_weight, w_embed, w_qkv, w_proj, w_up, w_down, w_unembed, norm_gains):
    side = N // PATCH
    state = image
    plain = jnp.zeros((side, side), jnp.int32)
    all_keep = jnp.ones((side, side), jnp.int32)
    index = jnp.arange(side, dtype=jnp.int32)
    for step in range(STEPS):
        grad = likelihood(state, gains, observed, vis_weight)
        half = state - STEP_SIZES[step] * grad
        patches = patches_of(half)
        tokens = jnp.dot(patches.reshape(side * side, PATCH * PATCH), w_embed, preferred_element_type=jnp.float32)
        tokens = tokens.astype(jnp.bfloat16).reshape(side, side, D)
        first = banded(tokens, plain, key_mask, w_qkv[0], w_proj[0], w_up[0], w_down[0], norm_gains[0])
        shift_rows = offsets[step, 0]
        shift_cols = offsets[step, 1]
        rolled = jnp.roll(first, -shift_rows, axis=0)
        rolled = jnp.roll(rolled, -shift_cols, axis=1)
        regions = 3 * region(index, shift_rows)[:, None] + region(index, shift_cols)[None, :]
        second = banded(rolled, regions, all_keep, w_qkv[1], w_proj[1], w_up[1], w_down[1], norm_gains[1])
        restored = jnp.roll(second, shift_rows, axis=0)
        restored = jnp.roll(restored, shift_cols, axis=1)
        estimate = jnp.dot(restored.reshape(side * side, D), w_unembed, preferred_element_type=jnp.float32)
        estimate = image_of(estimate.reshape(side, side, PATCH * PATCH))
        state = half - SIGMAS[step] * estimate + SIGMAS[step + 1] * noise[step]
    return state
```

```python
import functools
import math

import jax
import jax.numpy as jnp
import numpy as np
from jax import lax
from jax.experimental import pallas as pl
from jax.experimental.pallas import tpu as pltpu
from jax.sharding import PartitionSpec as P

N = 4096
WIN = 8
D = 512
HEADS = 8
FF = 2048
STEPS = 2
NTY = 16
NTX = 8
DEV = NTY * NTX
ROWS = 16
COLS = 32
TOKENS = ROWS * COLS
PIX = 256
SIDE = 256
SIGMAS = (0.8, 0.5, 0.3)
STEP_SIZES = (0.9, 0.7)
EPSILON = 1e-05
MESH = pl.DeviceIdType.MESH
F32 = jnp.float32
BF16 = jnp.bfloat16


def tables():
    k1 = np.array([32 * t + 16 * h + m for h in range(2) for t in range(8) for m in range(16)])
    k = np.arange(256)
    ang = 2 * np.pi * ((k1[:, None] * k[None, :]) % 256) / 256
    w1 = np.concatenate([np.cos(ang), -np.sin(ang)], axis=0)
    w4 = w1.T
    b = np.tile(np.arange(16), 16)
    ang = 2 * np.pi * (k1[:, None] * b[None, :]) / 4096
    tw1 = np.stack([np.cos(ang), np.sin(ang)])
    eye = np.eye(32)
    b16 = np.arange(16)
    ang = 2 * np.pi * ((b16[:, None] * b16[None, :]) % 16) / 16
    wr, wi = np.cos(ang), -np.sin(ang)
    core = np.zeros((2, 16, 16, 2))
    core[0, :, :, 0], core[0, :, :, 1] = wr, wi
    core[1, :, :, 0], core[1, :, :, 1] = -wi, wr
    core = core.reshape(2, 16, 8, 2, 2)
    f1 = np.einsum("cbpld,xy->cxbpdly", core, eye).reshape(1024, 1024)
    wi = -wi
    core = np.zeros((16, 2, 2, 16))
    core[:, 0, 0], core[:, 0, 1] = wr, wi
    core[:, 1, 0], core[:, 1, 1] = -wi, wr
    core = core.reshape(8, 2, 2, 2, 16)
    f2 = np.einsum("plcdb,xy->pclxdyb", core, eye).reshape(1024, 1024)
    u = np.arange(128)
    ang = 2 * np.pi * ((u[:, None] * u[None, :]) % 128) / 128
    w2 = np.concatenate([np.cos(ang), -np.sin(ang)], axis=1)
    w3 = np.concatenate([np.cos(ang), np.sin(ang)], axis=1)
    rho = np.arange(32)
    ang = 2 * np.pi * (rho[:, None] * u[None, :]) / 4096
    c, s = np.cos(ang), np.sin(ang)
    tw2c = np.concatenate([c, c, c, c], axis=0).T
    tw2s = np.concatenate([s, s, -s, -s], axis=0).T
    tw2 = np.stack([tw2c, tw2s])
    tw3 = np.stack([np.concatenate([c, c]), np.concatenate([s, s])]) / N
    ang = 2 * np.pi * ((rho[:, None] * rho[None, :]) % 32) / 32
    wr, wi = np.cos(ang), -np.sin(ang)
    eye2 = np.eye(2)

    def block(wr, wi):
        return np.block([[np.kron(eye2, wr), np.kron(eye2, -wi)], [np.kron(eye2, wi), np.kron(eye2, wr)]])

    m2 = block(wr, wi)
    m3 = block(wr, -wi)
    half = lambda x: np.asarray(x, np.float32).astype(BF16)
    full = lambda x: np.asarray(x, np.float32)
    return (half(w1), half(w4), full(tw1), half(f1), half(f2), half(w2), half(w3), full(tw2), full(tw3), half(m2), half(m3))


def mm(a, b):
    return jnp.dot(a, b, preferred_element_type=F32)


def nt(a, b):
    return lax.dot_general(a, b, (((1,), (1,)), ((), ())), preferred_element_type=F32)


def swap_blocks(x):
    sub = lax.broadcasted_iota(jnp.int32, x.shape, 1)
    lane = lax.broadcasted_iota(jnp.int32, x.shape, 2) // 16
    for d in (4, 2, 1):
        bs = (sub // d) % 2
        bl = (lane // d) % 2
        after = pltpu.roll(pltpu.roll(x, 8 - d, 1), 16 * d, 2)
        if d == 4:
            x = jnp.where(bs == bl, x, after)
        else:
            before = pltpu.roll(pltpu.roll(x, d, 1), 128 - 16 * d, 2)
            x = jnp.where(bs == bl, x, jnp.where(bs == 0, after, before))
    return x


def pixels_to_patches(read, write):
    for i in range(ROWS):
        pieces = [read(i * 16 + ah * 8, kh * 128) for kh in range(4) for ah in range(2)]
        out = swap_blocks(jnp.stack(pieces))
        for kh in range(4):
            for ah in range(2):
                write(i * COLS + kh * 8, ah * 128, out[kh * 2 + ah])


def patches_to_pixels(read, write):
    for i in range(ROWS):
        pieces = [read(i * COLS + kh * 8, ah * 128) for kh in range(4) for ah in range(2)]
        out = swap_blocks(jnp.stack(pieces))
        for kh in range(4):
            for ah in range(2):
                write(i * 16 + ah * 8, kh * 128, out[kh * 2 + ah])


def coords(d):
    return (d // NTX, lax.rem(d, NTX))


def exchange(mine, count, peer, src, dst, send_sem, recv_sem):
    def send(o, carry):
        t = lax.rem(mine + o, count)
        pltpu.make_async_remote_copy(
            src.at[t], dst.at[mine], send_sem, recv_sem, device_id=peer(t), device_id_type=MESH
        ).start()
        return carry

    lax.fori_loop(1, count, send, 0)
    dst[mine] = src[mine]
    rest = pltpu.make_async_remote_copy(
        src.at[pl.ds(0, count - 1)],
        dst.at[pl.ds(0, count - 1)],
        send_sem,
        recv_sem,
        device_id=peer(lax.rem(mine + 1, count)),
        device_id_type=MESH,
    )
    rest.wait_send()
    rest.wait_recv()


def layer_norm(values, gain):
    centre = jnp.mean(values, axis=-1, keepdims=True)
    shifted = values - centre
    spread = jnp.mean(shifted * shifted, axis=-1, keepdims=True)
    return shifted * lax.rsqrt(spread + EPSILON) * gain


def gelu(v):
    return 0.5 * v * (1.0 + jnp.tanh(math.sqrt(2.0 / math.pi) * (v + 0.044715 * (v * v * v))))


def swin_block(flow, qkv, att, allowed_of, w_qkv, w_proj, w_up, w_down, gains, j):
    gain0 = gains[j, 0:1, :]
    gain1 = gains[j, 1:2, :]
    normed = layer_norm(flow[...], gain0).astype(BF16)
    qkv[...] = mm(normed, w_qkv[j]).astype(BF16)
    lane_head = lax.broadcasted_iota(jnp.int32, (HEADS, 1, D), 2) // 64
    head = lax.broadcasted_iota(jnp.int32, (HEADS, 1, D), 0)
    own = lane_head == head
    own16 = jnp.where(own, 1.0, 0.0).astype(BF16)

    def window(w, carry):
        rows = pl.ds(pl.multiple_of(w * 64, 64), 64)
        q = qkv[rows, 0:D]
        k = qkv[rows, D : 2 * D]
        v = qkv[rows, 2 * D : 3 * D]
        spread_q = (q[None] * own16).reshape(HEADS * 64, D)
        scores = nt(spread_q, k).reshape(HEADS, 64, 64) * 0.125
        scores = jnp.where(allowed_of(w)[None], scores, -1e30)
        largest = jnp.max(scores, axis=-1, keepdims=True)
        weights = jnp.exp(scores - largest)
        probs = (weights / jnp.sum(weights, axis=-1, keepdims=True)).astype(BF16)
        mixed = mm(probs.reshape(HEADS * 64, 64), v).reshape(HEADS, 64, D)
        att[rows, :] = jnp.sum(jnp.where(own, mixed, 0.0), axis=0).astype(BF16)
        return carry

    lax.fori_loop(0, 8, window, 0)
    after = flow[...] + mm(att[...], w_proj[j])
    normed = layer_norm(after, gain1).astype(BF16)
    for c in range(0, FF, 512):
        hidden = gelu(mm(normed, w_up[j, :, c : c + 512])).astype(BF16)
        after = after + mm(hidden, w_down[j, c : c + 512, :])
    flow[...] = after


def region(index, shift):
    return jnp.where(index < SIDE - WIN, 0, jnp.where(index < SIDE - shift, 1, 2))


def windows():
    return [(wi, wk, p, ((wi * 4 + wk) * 8 + p) * 8) for wi in range(2) for wk in range(4) for p in range(8)]


def kernel(
    offsets, image, noise, keep, norm_gains,
    w1, w4, tw1, w2, w3, tw2, tw3, m2, m3,
    gains_h, observed_h, weight_h, f1_h, f2_h, w_embed_h, w_qkv_h, w_proj_h, w_up_h, w_down_h, w_unembed_h,
    out,
    gains, observed, weight, f1, f2, w_embed, w_qkv, w_proj, w_up, w_down, w_unembed,
    state, half, sa, ra, sb, rb, sc, rc, sd, rd, xf, xg, big, abr, flow, qkv, att, first, padded, around,
    from_right, from_below, from_corner, to_right, to_below, to_corner, est,
    load_sem, send_sem, recv_sem,
):
    ty = lax.axis_index("ty")
    tx = lax.axis_index("tx")
    me = ty * NTX + tx
    barrier = pltpu.get_barrier_semaphore()

    def greet(o, carry):
        pl.semaphore_signal(barrier, inc=1, device_id=coords(lax.rem(me + o, DEV)), device_id_type=MESH)
        return carry

    lax.fori_loop(1, DEV, greet, 0)
    pairs = [
        (f1_h, f1), (gains_h, gains), (observed_h, observed), (weight_h, weight), (f2_h, f2), (w_embed_h, w_embed),
        (w_qkv_h, w_qkv), (w_proj_h, w_proj), (w_up_h, w_up), (w_down_h, w_down), (w_unembed_h, w_unembed),
    ]
    loads = [pltpu.make_async_copy(a, b, load_sem.at[n]) for n, (a, b) in enumerate(pairs)]
    for load in loads:
        load.start()

    def put_state(row, lane, piece):
        state[row : row + 8, lane : lane + 128] = piece

    pixels_to_patches(lambda r, c: image[r : r + 8, c : c + 128], put_state)
    lane = lax.broadcasted_iota(jnp.int32, (128, 128), 1)
    low = (lane // 32) % 2 == 0
    sign = jnp.where(lane < 64, -1.0, 1.0)
    right = lax.rem(tx + 1, NTX)
    left = lax.rem(tx + NTX - 1, NTX)
    below = lax.rem(ty + 1, NTY)
    above = lax.rem(ty + NTY - 1, NTY)

    for t in range(STEPS):
        base = t * 10

        sa[...] = state[...].astype(BF16).reshape(NTX, 64, PIX)
        if t == 0:
            pl.semaphore_wait(barrier, DEV - 1)
        exchange(tx, NTX, lambda n: (ty, n), sa, ra.at[t], send_sem.at[base], recv_sem.at[base])
        got = ra[t]
        slab = jnp.concatenate([got[:, :32, :].reshape(256, PIX), got[:, 32:, :].reshape(256, PIX)], axis=1)
        cos1 = jnp.concatenate([tw1[0], tw1[0]], axis=1)
        sin1 = jnp.concatenate([tw1[1], tw1[1]], axis=1)
        part = mm(w1[...], slab)
        pr, pi = part[:256], part[256:]
        part = jnp.concatenate([pr * cos1 + pi * sin1, pi * cos1 - pr * sin1], axis=1).astype(BF16)
        if t == 0:
            loads[0].wait()
        big[...] = mm(part, f1[...])
        for p in range(8):
            a0 = big[0:128, p * 128 : p * 128 + 128]
            a1 = big[128:256, p * 128 : p * 128 + 128]
            sb[p * 16 : p * 16 + 8] = jnp.where(low, a0, pltpu.roll(a1, 32, 1)).astype(BF16).reshape(8, 16, 128)
            sb[p * 16 + 8 : p * 16 + 16] = jnp.where(low, pltpu.roll(a0, 96, 1), a1).astype(BF16).reshape(8, 16, 128)
        exchange(me, DEV, coords, sb, rb.at[t], send_sem.at[base + 1], recv_sem.at[base + 1])

        if t == 0:
            for n in (1, 2, 3):
                loads[n].wait()
            for q in range(4):
                rows = slice(q * 8, q * 8 + 8)
                for v in range(32):
                    cols = slice(v * 128, v * 128 + 128)
                    gr, gi = gains[0, rows, cols], gains[1, rows, cols]
                    zr, zi = observed[0, rows, cols], observed[1, rows, cols]
                    wt = weight[rows, cols]
                    at = slice((q * 32 + v) * 8, (q * 32 + v) * 8 + 8)
                    xf[at, :] = (wt * (gr * gr + gi * gi)) * (1.0 / N)
                    xf[1024 + at.start : 1024 + at.stop, :] = wt * (gr * zr + gi * zi)
                    xg[at, :] = wt * (gr * zi - gi * zr)
            for q in range(4):
                h, mh = q // 2, q % 2
                for ml in range(8):
                    cols = slice((mh * 8 + ml) * 128, (mh * 8 + ml) * 128 + 128)
                    abr[0, h * 32 : h * 32 + 32, cols] = xf[pl.ds(q * 256 + ml, 32, stride=8), :]
                    abr[1, h * 32 : h * 32 + 32, cols] = xf[pl.ds(1024 + q * 256 + ml, 32, stride=8), :]
                    abr[2, h * 32 : h * 32 + 32, cols] = xg[pl.ds(q * 256 + ml, 32, stride=8), :]

        xf[...] = rb[t].reshape(DEV * 16, 128).astype(F32)
        for m4 in range(0, 16, 4):
            xs = [xf[pl.ds(m4 + n, DEV, stride=16), :] for n in range(4)]
            turned = [pltpu.roll(x, 64, 1) * sign for x in xs]
            both = jnp.concatenate([jnp.concatenate(xs, axis=1), jnp.concatenate(turned, axis=1)], axis=0).astype(BF16)
            y = mm(w2[...], both)
            ys = [y[:, n * 128 : n * 128 + 128] for n in range(4)]
            ys = [x * tw2[0] + pltpu.roll(x, 64, 1) * tw2[1] for x in ys]
            z = nt(m2[...], jnp.concatenate(ys, axis=0).astype(BF16))
            cols = slice(m4 * 128, m4 * 128 + 512)
            fac = abr[0, :, cols]
            back = jnp.concatenate([fac * z[:64] - abr[1, :, cols], fac * z[64:] - abr[2, :, cols]], axis=0)
            v = mm(m3[...], back.astype(BF16))
            rows = []
            for n in range(4):
                vr, vi = v[:64, n * 128 : n * 128 + 128], v[64:, n * 128 : n * 128 + 128]
                xr = vr * tw3[0] - vi * tw3[1]
                xi = vi * tw3[0] + vr * tw3[1]
                rows.append(jnp.concatenate([jnp.concatenate([xr, xi], axis=0), jnp.concatenate([-xi, xr], axis=0)], axis=1))
            u = nt(w3[...], jnp.concatenate(rows, axis=0).astype(BF16))
            for n in range(4):
                xf[pl.ds(m4 + n, DEV, stride=16), :] = u[:, n * 128 : n * 128 + 128]
        sc[...] = xf[...].astype(BF16).reshape(DEV, 16, 128)
        exchange(me, DEV, coords, sc, rc.at[t], send_sem.at[base + 2], recv_sem.at[base + 2])

        for p in range(8):
            r0 = rc[t, p * 16 : p * 16 + 8].reshape(128, 128).astype(F32)
            r1 = rc[t, p * 16 + 8 : p * 16 + 16].reshape(128, 128).astype(F32)
            big[0:128, p * 128 : p * 128 + 128] = jnp.where(low, r0, pltpu.roll(r1, 32, 1))
            big[128:256, p * 128 : p * 128 + 128] = jnp.where(low, pltpu.roll(r0, 96, 1), r1)
        if t == 0:
            loads[4].wait()
        part = mm(big[...].astype(BF16), f2[...])
        pr, pi = part[:, :512], part[:, 512:]
        part = jnp.concatenate([pr * cos1 - pi * sin1, pi * cos1 + pr * sin1], axis=0)
        y = mm(w4[...], part.astype(BF16)).astype(BF16)
        for n in range(NTX):
            sd[n, 0:32, :] = y[n * 32 : n * 32 + 32, :PIX]
            sd[n, 32:64, :] = y[n * 32 : n * 32 + 32, PIX:]
        exchange(tx, NTX, lambda n: (ty, n), sd, rd.at[t], send_sem.at[base + 3], recv_sem.at[base + 3])
        half[...] = state[...] - STEP_SIZES[t] * rd[t].reshape(TOKENS, PIX).astype(F32)

        if t == 0:
            for n in (5, 6, 7, 8, 9, 10):
                loads[n].wait()
        for wi, wk, p, row in windows():
            at = (wi * 8 + p) * COLS + wk * 8
            est[row : row + 8, :] = half[at : at + 8, :]
        flow[...] = mm(est[...].astype(BF16), w_embed[...]).astype(BF16).astype(F32)

        def kept(w):
            row = lax.broadcasted_iota(jnp.int32, (64, 64), 0)
            col = lax.broadcasted_iota(jnp.int32, (64, 64), 1)
            return (keep[pl.ds(w, 1), :] == 1) | (row == col)

        swin_block(flow, qkv, att, kept, w_qkv, w_proj, w_up, w_down, norm_gains, 0)
        first[...] = flow[...].astype(BF16)
        sr = offsets[t, 0]
        sc_ = offsets[t, 1]
        sends = []

        def send(src, dst, who, n):
            copy = pltpu.make_async_remote_copy(
                src, dst, send_sem.at[base + n], recv_sem.at[base + n], device_id=who, device_id_type=MESH
            )
            copy.start()
            sends.append(copy)

        send(first.at[pl.ds(0, 256)], from_below.at[t], (above, tx), 4)
        att[0:64, :] = first[0:64, :]
        att[64:128, :] = first[256:320, :]
        send(att.at[pl.ds(0, 128)], from_right.at[t], (ty, left), 5)
        send(first.at[pl.ds(0, 64)], from_corner.at[t], (above, left), 6)
        for wi, wk, p, row in windows():
            padded[wi * 8 + p, wk * 8 : wk * 8 + 8, :] = first[row : row + 8, :].astype(F32)
        for copy in sends:
            copy.wait()
        for wi, wk, p, row in windows():
            if wi == 0:
                padded[16 + p, wk * 8 : wk * 8 + 8, :] = from_below[t, row : row + 8, :].astype(F32)
            if wk == 0:
                at = (wi * 8 + p) * 8
                padded[wi * 8 + p, 32:40, :] = from_right[t, at : at + 8, :].astype(F32)
            if wi == 0 and wk == 0:
                padded[16 + p, 32:40, :] = from_corner[t, row : row + 8, :].astype(F32)
        for i in range(ROWS):
            rolled = pltpu.roll(padded[i + sr], COLS + 8 - sc_, 0)
            for wk in range(4):
                row = ((i // 8 * 4 + wk) * 8 + i % 8) * 8
                flow[row : row + 8, :] = rolled[wk * 8 : wk * 8 + 8, :]

        def same(w):
            wi = w // 4
            wk = lax.rem(w, 4)
            row = lax.broadcasted_iota(jnp.int32, (64, 64), 0)
            col = lax.broadcasted_iota(jnp.int32, (64, 64), 1)

            def label(x):
                i = ty * ROWS + wi * 8 + x // 8
                k = tx * COLS + wk * 8 + x % 8
                return 3 * region(i, sr) + region(k, sc_)

            return label(row) == label(col)

        swin_block(flow, qkv, att, same, w_qkv, w_proj, w_up, w_down, norm_gains, 1)
        est[...] = mm(flow[...].astype(BF16), w_unembed[...])
        sends.clear()
        sa.reshape(TOKENS, PIX)[...] = est[...].astype(BF16)
        for wi, wk, p, row in windows():
            around[8 + wi * 8 + p, 8 + wk * 8 : 16 + wk * 8, :] = est[row : row + 8, :]
        sd[0] = sa[3]
        sd[1] = sa[7]
        send(sd.at[pl.ds(0, 2)], to_right.at[t], (ty, right), 7)
        send(sa.at[pl.ds(4, 4)], to_below.at[t], (below, tx), 8)
        send(sa.at[7], to_corner.at[t], (below, right), 9)
        for copy in sends:
            copy.wait()
        for p in range(8):
            for wi in range(2):
                around[8 + wi * 8 + p, 0:8, :] = to_right[t, wi, p * 8 : p * 8 + 8, :].astype(F32)
            for wk in range(4):
                around[p, 8 + wk * 8 : 16 + wk * 8, :] = to_below[t, wk, p * 8 : p * 8 + 8, :].astype(F32)
            around[p, 0:8, :] = to_corner[t, p * 8 : p * 8 + 8, :].astype(F32)
        for i in range(ROWS):
            rows = slice(i * COLS, i * COLS + COLS)
            piece = pltpu.roll(around[8 + i - sr], COLS + sc_, 0)[:COLS]
            state[rows, :] = half[rows, :] - SIGMAS[t] * piece
        if t + 1 < STEPS:

            def add_noise(row, lane, piece):
                state[row : row + 8, lane : lane + 128] = state[row : row + 8, lane : lane + 128] + SIGMAS[t + 1] * piece

            pixels_to_patches(lambda r, c: noise[t, r : r + 8, c : c + 128], add_noise)
        else:

            def give(row, lane, piece):
                out[row : row + 8, lane : lane + 128] = piece + SIGMAS[t + 1] * noise[t, row : row + 8, lane : lane + 128]

            patches_to_pixels(lambda r, c: state[r : r + 8, c : c + 128], give)


def per_device(consts, image, noise, offsets, key_mask, gains, observed, vis_weight, w_embed, w_qkv, w_proj, w_up, w_down, w_unembed, norm_gains):
    w1, w4, tw1, f1, f2, w2, w3, tw2, tw3, m2, m3 = consts
    keep = key_mask.reshape(2, 8, 4, 8).transpose(0, 2, 1, 3).reshape(8, 64)
    vmem = pl.BlockSpec(memory_space=pltpu.VMEM)
    hbm = pl.BlockSpec(memory_space=pl.ANY)
    smem = pl.BlockSpec(memory_space=pltpu.SMEM)
    moved = (gains, observed, vis_weight, f1, f2, w_embed, w_qkv, w_proj, w_up, w_down, w_unembed)
    held = [pltpu.VMEM(x.shape, x.dtype) for x in moved]
    V = pltpu.VMEM
    scratch = held + [
        V((TOKENS, PIX), F32),
        V((TOKENS, PIX), F32),
        V((NTX, 64, PIX), BF16),
        V((STEPS, NTX, 64, PIX), BF16),
        V((DEV, 16, 128), BF16),
        V((STEPS, DEV, 16, 128), BF16),
        V((DEV, 16, 128), BF16),
        V((STEPS, DEV, 16, 128), BF16),
        V((NTX, 64, PIX), BF16),
        V((STEPS, NTX, 64, PIX), BF16),
        V((DEV * 16, 128), F32),
        V((1024, 128), F32),
        V((256, 1024), F32),
        V((3, 64, 2048), F32),
        V((TOKENS, D), F32),
        V((TOKENS, 3 * D), BF16),
        V((TOKENS, D), BF16),
        V((TOKENS, D), BF16),
        V((ROWS + 8, COLS + 8, D), F32),
        V((ROWS + 8, COLS + 8, PIX), F32),
        V((STEPS, 128, D), BF16),
        V((STEPS, 256, D), BF16),
        V((STEPS, 64, D), BF16),
        V((STEPS, 2, 64, PIX), BF16),
        V((STEPS, 4, 64, PIX), BF16),
        V((STEPS, 64, PIX), BF16),
        V((TOKENS, PIX), F32),
        pltpu.SemaphoreType.DMA((len(moved),)),
        pltpu.SemaphoreType.DMA((STEPS * 10,)),
        pltpu.SemaphoreType.DMA((STEPS * 10,)),
    ]
    return pl.pallas_call(
        kernel,
        out_shape=jax.ShapeDtypeStruct(image.shape, F32),
        in_specs=[smem] + [vmem] * 13 + [hbm] * len(moved),
        out_specs=vmem,
        scratch_shapes=scratch,
        compiler_params=pltpu.CompilerParams(collective_id=0, has_side_effects=True, vmem_limit_bytes=60 * 2**20),
    )(
        offsets, image, noise, keep, norm_gains,
        w1, w4, tw1, w2, w3, tw2, tw3, m2, m3,
        *moved,
    )


def solution(mesh):
    consts = tables()
    in_specs = (
        P("ty", "tx"),
        P(None, "ty", "tx"),
        P(),
        P("ty", "tx"),
        P(None, ("ty", "tx"), None),
        P(None, ("ty", "tx"), None),
        P(("ty", "tx"), None),
        P(),
        P(),
        P(),
        P(),
        P(),
        P(),
        P(),
    )
    consts_specs = (P(),) * len(consts)
    mapped = jax.shard_map(
        lambda c, *args: per_device(c, *args),
        mesh=mesh,
        in_specs=(consts_specs,) + in_specs,
        out_specs=P("ty", "tx"),
        check_vma=False,
    )
    return lambda *args: mapped(tuple(jnp.asarray(c) for c in consts), *args)
```

```python
import functools
import math

import jax
import jax.numpy as jnp
import numpy as np
from jax import lax
from jax.experimental import pallas as pl
from jax.experimental.pallas import tpu as pltpu
from jax.sharding import PartitionSpec as P

N = 4096
WIN = 8
D = 512
HEADS = 8
FF = 2048
STEPS = 2
NTY = 16
NTX = 8
DEV = NTY * NTX
ROWS = 16
COLS = 32
TOKENS = ROWS * COLS
PIX = 256
SIDE = 256
SIGMAS = (0.8, 0.5, 0.3)
STEP_SIZES = (0.9, 0.7)
EPSILON = 1e-05
MESH = pl.DeviceIdType.MESH
F32 = jnp.float32
BF16 = jnp.bfloat16


def tables():
    k1 = np.array([32 * t + 16 * h + m for h in range(2) for t in range(8) for m in range(16)])
    k = np.arange(256)
    ang = 2 * np.pi * ((k1[:, None] * k[None, :]) % 256) / 256
    w1 = np.concatenate([np.cos(ang), -np.sin(ang)], axis=0)
    w4 = w1.T
    b = np.tile(np.arange(16), 16)
    ang = 2 * np.pi * (k1[:, None] * b[None, :]) / 4096
    tw1 = np.stack([np.cos(ang), np.sin(ang)])
    eye = np.eye(32)
    b16 = np.arange(16)
    ang = 2 * np.pi * ((b16[:, None] * b16[None, :]) % 16) / 16
    wr, wi = np.cos(ang), -np.sin(ang)
    core = np.zeros((2, 16, 16, 2))
    core[0, :, :, 0], core[0, :, :, 1] = wr, wi
    core[1, :, :, 0], core[1, :, :, 1] = -wi, wr
    core = core.reshape(2, 16, 8, 2, 2)
    f1 = np.einsum("cbpld,xy->cxbpdly", core, eye).reshape(1024, 1024)
    wi = -wi
    core = np.zeros((16, 2, 2, 16))
    core[:, 0, 0], core[:, 0, 1] = wr, wi
    core[:, 1, 0], core[:, 1, 1] = -wi, wr
    core = core.reshape(8, 2, 2, 2, 16)
    f2 = np.einsum("plcdb,xy->pclxdyb", core, eye).reshape(1024, 1024)
    u = np.arange(128)
    ang = 2 * np.pi * ((u[:, None] * u[None, :]) % 128) / 128
    w2 = np.concatenate([np.cos(ang), -np.sin(ang)], axis=1)
    w3 = np.concatenate([np.cos(ang), np.sin(ang)], axis=1)
    rho = np.arange(32)
    ang = 2 * np.pi * (rho[:, None] * u[None, :]) / 4096
    c, s = np.cos(ang), np.sin(ang)
    tw2c = np.concatenate([c, c, c, c], axis=0).T
    tw2s = np.concatenate([s, s, -s, -s], axis=0).T
    tw2 = np.stack([tw2c, tw2s])
    tw3 = np.stack([np.concatenate([c, c]), np.concatenate([s, s])]) / N
    ang = 2 * np.pi * ((rho[:, None] * rho[None, :]) % 32) / 32
    wr, wi = np.cos(ang), -np.sin(ang)
    eye2 = np.eye(2)

    def block(wr, wi):
        return np.block([[np.kron(eye2, wr), np.kron(eye2, -wi)], [np.kron(eye2, wi), np.kron(eye2, wr)]])

    m2 = block(wr, wi)
    m3 = block(wr, -wi)
    half = lambda x: np.asarray(x, np.float32).astype(BF16)
    full = lambda x: np.asarray(x, np.float32)
    return (half(w1), half(w4), full(tw1), half(f1), half(f2), half(w2), half(w3), full(tw2), full(tw3), half(m2), half(m3))


def mm(a, b):
    return jnp.dot(a, b, preferred_element_type=F32)


def nt(a, b):
    return lax.dot_general(a, b, (((1,), (1,)), ((), ())), preferred_element_type=F32)


def swap_blocks(x):
    sub = lax.broadcasted_iota(jnp.int32, x.shape, 1)
    lane = lax.broadcasted_iota(jnp.int32, x.shape, 2) // 16
    for d in (4, 2, 1):
        bs = (sub // d) % 2
        bl = (lane // d) % 2
        after = pltpu.roll(pltpu.roll(x, 8 - d, 1), 16 * d, 2)
        if d == 4:
            x = jnp.where(bs == bl, x, after)
        else:
            before = pltpu.roll(pltpu.roll(x, d, 1), 128 - 16 * d, 2)
            x = jnp.where(bs == bl, x, jnp.where(bs == 0, after, before))
    return x


def pixels_to_patches(read, write):
    for i in range(ROWS):
        pieces = [read(i * 16 + ah * 8, kh * 128) for kh in range(4) for ah in range(2)]
        out = swap_blocks(jnp.stack(pieces))
        for kh in range(4):
            for ah in range(2):
                write(i * COLS + kh * 8, ah * 128, out[kh * 2 + ah])


def patches_to_pixels(read, write):
    for i in range(ROWS):
        pieces = [read(i * COLS + kh * 8, ah * 128) for kh in range(4) for ah in range(2)]
        out = swap_blocks(jnp.stack(pieces))
        for kh in range(4):
            for ah in range(2):
                write(i * 16 + ah * 8, kh * 128, out[kh * 2 + ah])


def coords(d):
    return (d // NTX, lax.rem(d, NTX))


def begin(mine, count, peer, src, dst, send_sem, recv_sem):
    def send(o, carry):
        t = lax.rem(mine + o, count)
        pltpu.make_async_remote_copy(
            src.at[t], dst.at[mine], send_sem, recv_sem, device_id=peer(t), device_id_type=MESH
        ).start()
        return carry

    lax.fori_loop(1, count, send, 0)
    dst[mine] = src[mine]

    def finish():
        rest = pltpu.make_async_remote_copy(
            src.at[pl.ds(0, count - 1)],
            dst.at[pl.ds(0, count - 1)],
            send_sem,
            recv_sem,
            device_id=peer(lax.rem(mine + 1, count)),
            device_id_type=MESH,
        )
        rest.wait_send()
        rest.wait_recv()

    return finish


def exchange(*args):
    begin(*args)()


def layer_norm(values, gain):
    centre = jnp.mean(values, axis=-1, keepdims=True)
    shifted = values - centre
    spread = jnp.mean(shifted * shifted, axis=-1, keepdims=True)
    return shifted * lax.rsqrt(spread + EPSILON) * gain


def gelu(v):
    return 0.5 * v * (1.0 + jnp.tanh(math.sqrt(2.0 / math.pi) * (v + 0.044715 * (v * v * v))))


def swin_rows(flow, qkv, att, start, count, bias_of, w_qkv, w_proj, w_up, w_down, gains, j):
    rows = slice(start * 64, (start + count) * 64)
    normed = layer_norm(flow[rows, :], gains[j, 0:1, :]).astype(BF16)
    qkv[rows, :] = mm(normed, w_qkv[j]).astype(BF16)
    lane = lax.broadcasted_iota(jnp.int32, (1, 128), 1)
    low = lane < 64
    pick_low = jnp.where(low, 0.125, 0.0).astype(BF16)
    pick_high = jnp.where(low, 0.0, 0.125).astype(BF16)
    for n in range(start, start + count):
        at = slice(n * 64, n * 64 + 64)
        bias = bias_of(n)
        for pair in range(4):
            cols = slice(pair * 128, pair * 128 + 128)
            q = qkv[at, cols]
            k = qkv[at, D + pair * 128 : D + pair * 128 + 128]
            v = qkv[at, 2 * D + pair * 128 : 2 * D + pair * 128 + 128]
            both = jnp.concatenate([q * pick_low, q * pick_high], axis=0)
            scores = nt(both, k) + bias
            weights = jnp.exp(scores - jnp.max(scores, axis=1, keepdims=True))
            probs = weights * (1.0 / jnp.sum(weights, axis=1, keepdims=True))
            mixed = mm(probs.astype(BF16), v)
            att[at, cols] = jnp.where(low, mixed[:64], mixed[64:]).astype(BF16)
    after = flow[rows, :] + mm(att[rows, :], w_proj[j])
    normed = layer_norm(after, gains[j, 1:2, :]).astype(BF16)
    for c in range(0, FF, 512):
        hidden = gelu(mm(normed, w_up[j, :, c : c + 512])).astype(BF16)
        after = after + mm(hidden, w_down[j, c : c + 512, :])
    flow[rows, :] = after


def region(index, shift):
    return jnp.where(index < SIDE - WIN, 0, jnp.where(index < SIDE - shift, 1, 2))


NAMES = (
    "image", "key_mask", "w1", "tw1", "f1", "gains", "observed", "weight", "w2", "w3", "tw2", "tw3", "m2", "m3", "f2", "w4",
    "norm_gains", "w_embed", "w_qkv", "w_proj", "w_up", "w_down", "w_unembed", "noise",
)


def kernel(offsets, *refs):
    count = len(NAMES)
    sources = refs[:count]
    out = refs[count]
    held = refs[count + 1 : 2 * count + 1]
    (
        image, key_mask, w1, tw1, f1, gains, observed, weight, w2, w3, tw2, tw3, m2, m3, f2, w4,
        norm_gains, w_embed, w_qkv, w_proj, w_up, w_down, w_unembed, noise,
    ) = held
    (
        state, half, sa, ra, sb, rb, sc, rc, sd, rd, xf, xg, big, abr, flow, qkv, att, first, padded, around,
        from_right, from_below, from_corner, to_right, to_below, to_corner, bias0, load_sem, send_sem, recv_sem,
    ) = refs[2 * count + 1 :]
    ty = lax.axis_index("ty")
    tx = lax.axis_index("tx")
    me = ty * NTX + tx
    barrier = pltpu.get_barrier_semaphore()

    def greet(o, carry):
        pl.semaphore_signal(barrier, inc=1, device_id=coords(lax.rem(me + o, DEV)), device_id_type=MESH)
        return carry

    lax.fori_loop(1, DEV, greet, 0)
    loads = {}
    for n, name in enumerate(NAMES):
        source = sources[n].at[0] if name == "noise" else sources[n]
        loads[name] = pltpu.make_async_copy(source, held[n], load_sem.at[n])
        loads[name].start()

    def need(*names):
        for name in names:
            if name in loads:
                loads.pop(name).wait()

    need("image")

    def put_state(row, lane, piece):
        state[row : row + 8, lane : lane + 128] = piece

    pixels_to_patches(lambda r, c: image[r : r + 8, c : c + 128], put_state)
    lane = lax.broadcasted_iota(jnp.int32, (128, 128), 1)
    low = (lane // 32) % 2 == 0
    sign = jnp.where(lane < 64, -1.0, 1.0)
    right = lax.rem(tx + 1, NTX)
    left = lax.rem(tx + NTX - 1, NTX)
    below = lax.rem(ty + 1, NTY)
    above = lax.rem(ty + NTY - 1, NTY)

    need("key_mask")
    key = lax.broadcasted_iota(jnp.int32, (1, 64), 1)
    query = lax.broadcasted_iota(jnp.int32, (128, 1), 0) % 64
    spot = lax.broadcasted_iota(jnp.int32, (64, 1), 0)
    mask_lane = lax.broadcasted_iota(jnp.int32, (64, COLS), 1)
    for w in range(8):
        wk, wi = w // 2, w % 2
        lines = [jnp.broadcast_to(key_mask[wi * 8 + p : wi * 8 + p + 1, :], (8, COLS)) for p in range(8)]
        lines = jnp.concatenate(lines, axis=0)
        kept = jnp.sum(jnp.where(mask_lane == wk * 8 + spot % 8, lines, 0).astype(F32), axis=1, keepdims=True)
        kept = jnp.sum(jnp.where(spot == key, kept, 0.0), axis=0, keepdims=True)
        bias0[w] = jnp.where((kept == 1.0) | (key == query), 0.0, -1e30)

    for t in range(STEPS):
        base = t * 16

        sa[...] = state[...].astype(BF16).reshape(NTX, 64, PIX)
        if t == 0:
            pl.semaphore_wait(barrier, DEV - 1)
        exchange(tx, NTX, lambda n: (ty, n), sa, ra.at[t], send_sem.at[base], recv_sem.at[base])
        got = ra[t]
        slab = jnp.concatenate([got[:, :32, :].reshape(256, PIX), got[:, 32:, :].reshape(256, PIX)], axis=1)
        need("w1", "tw1")
        cos1 = jnp.concatenate([tw1[0], tw1[0]], axis=1)
        sin1 = jnp.concatenate([tw1[1], tw1[1]], axis=1)
        part = mm(w1[...], slab)
        pr, pi = part[:256], part[256:]
        part = jnp.concatenate([pr * cos1 + pi * sin1, pi * cos1 - pr * sin1], axis=1).astype(BF16)
        need("f1")
        big[...] = mm(part, f1[...])
        for p in range(8):
            a0 = big[0:128, p * 128 : p * 128 + 128]
            a1 = big[128:256, p * 128 : p * 128 + 128]
            sb[p * 16 : p * 16 + 8] = jnp.where(low, a0, pltpu.roll(a1, 32, 1)).astype(BF16).reshape(8, 16, 128)
            sb[p * 16 + 8 : p * 16 + 16] = jnp.where(low, pltpu.roll(a0, 96, 1), a1).astype(BF16).reshape(8, 16, 128)
        exchange(me, DEV, coords, sb, rb.at[t], send_sem.at[base + 1], recv_sem.at[base + 1])

        if t == 0:
            need("gains", "observed", "weight", "w2", "w3", "tw2", "tw3", "m2", "m3")
            for q in range(4):
                rows = slice(q * 8, q * 8 + 8)
                for v in range(32):
                    cols = slice(v * 128, v * 128 + 128)
                    gr, gi = gains[0, rows, cols], gains[1, rows, cols]
                    zr, zi = observed[0, rows, cols], observed[1, rows, cols]
                    wt = weight[rows, cols]
                    at = slice((q * 32 + v) * 8, (q * 32 + v) * 8 + 8)
                    xf[at, :] = (wt * (gr * gr + gi * gi)) * (1.0 / N)
                    xf[1024 + at.start : 1024 + at.stop, :] = wt * (gr * zr + gi * zi)
                    xg[at, :] = wt * (gr * zi - gi * zr)
            for q in range(4):
                h, mh = q // 2, q % 2
                for ml in range(8):
                    cols = slice((mh * 8 + ml) * 128, (mh * 8 + ml) * 128 + 128)
                    abr[0, h * 32 : h * 32 + 32, cols] = xf[pl.ds(q * 256 + ml, 32, stride=8), :]
                    abr[1, h * 32 : h * 32 + 32, cols] = xf[pl.ds(1024 + q * 256 + ml, 32, stride=8), :]
                    abr[2, h * 32 : h * 32 + 32, cols] = xg[pl.ds(q * 256 + ml, 32, stride=8), :]

        xf[...] = rb[t].reshape(DEV * 16, 128).astype(F32)
        for m4 in range(0, 16, 4):
            xs = [xf[pl.ds(m4 + n, DEV, stride=16), :] for n in range(4)]
            turned = [pltpu.roll(x, 64, 1) * sign for x in xs]
            both = jnp.concatenate([jnp.concatenate(xs, axis=1), jnp.concatenate(turned, axis=1)], axis=0).astype(BF16)
            y = mm(w2[...], both)
            ys = [y[:, n * 128 : n * 128 + 128] for n in range(4)]
            ys = [x * tw2[0] + pltpu.roll(x, 64, 1) * tw2[1] for x in ys]
            z = nt(m2[...], jnp.concatenate(ys, axis=0).astype(BF16))
            cols = slice(m4 * 128, m4 * 128 + 512)
            fac = abr[0, :, cols]
            back = jnp.concatenate([fac * z[:64] - abr[1, :, cols], fac * z[64:] - abr[2, :, cols]], axis=0)
            v = mm(m3[...], back.astype(BF16))
            rows = []
            for n in range(4):
                vr, vi = v[:64, n * 128 : n * 128 + 128], v[64:, n * 128 : n * 128 + 128]
                xr = vr * tw3[0] - vi * tw3[1]
                xi = vi * tw3[0] + vr * tw3[1]
                rows.append(jnp.concatenate([jnp.concatenate([xr, xi], axis=0), jnp.concatenate([-xi, xr], axis=0)], axis=1))
            u = nt(w3[...], jnp.concatenate(rows, axis=0).astype(BF16))
            for n in range(4):
                xf[pl.ds(m4 + n, DEV, stride=16), :] = u[:, n * 128 : n * 128 + 128]
        sc[...] = xf[...].astype(BF16).reshape(DEV, 16, 128)
        exchange(me, DEV, coords, sc, rc.at[t], send_sem.at[base + 2], recv_sem.at[base + 2])

        for p in range(8):
            r0 = rc[t, p * 16 : p * 16 + 8].reshape(128, 128).astype(F32)
            r1 = rc[t, p * 16 + 8 : p * 16 + 16].reshape(128, 128).astype(F32)
            big[0:128, p * 128 : p * 128 + 128] = jnp.where(low, r0, pltpu.roll(r1, 32, 1))
            big[128:256, p * 128 : p * 128 + 128] = jnp.where(low, pltpu.roll(r0, 96, 1), r1)
        need("f2", "w4")
        part = mm(big[...].astype(BF16), f2[...])
        pr, pi = part[:, :512], part[:, 512:]
        part = jnp.concatenate([pr * cos1 - pi * sin1, pi * cos1 + pr * sin1], axis=0)
        part = part.astype(BF16)

        gradient = []
        for hf in range(2):
            for n in range(NTX):
                y = mm(w4[n * 32 + hf * 16 : n * 32 + hf * 16 + 16, :], part).astype(BF16)
                sd[hf, n, 0:16, :] = y[:, :PIX]
                sd[hf, n, 16:32, :] = y[:, PIX:]
            gradient.append(
                begin(tx, NTX, lambda n: (ty, n), sd.at[hf], rd.at[t, hf], send_sem.at[base + 3 + hf], recv_sem.at[base + 3 + hf])
            )

        need("w_embed", "w_qkv", "w_proj", "w_up", "w_down", "w_unembed", "norm_gains")
        sr = offsets[t, 0]
        sc_ = offsets[t, 1]
        sends = []

        def send(src, dst, who, n):
            copy = pltpu.make_async_remote_copy(
                src, dst, send_sem.at[base + n], recv_sem.at[base + n], device_id=who, device_id_type=MESH
            )
            copy.start()
            sends.append(copy)

        for hf in range(2):
            gradient[hf]()
            grad = rd[t, hf].astype(F32)
            pieces = []
            for w in range(hf * 4, hf * 4 + 4):
                wk, wi = w // 2, w % 2
                for p in range(8):
                    i = wi * 8 + p
                    at = i * COLS + wk * 8
                    move = grad[i // 2, (i % 2) * 16 + (wk % 2) * 8 : (i % 2) * 16 + (wk % 2) * 8 + 8, :]
                    piece = state[at : at + 8, :] - STEP_SIZES[t] * move
                    half[at : at + 8, :] = piece
                    pieces.append(piece)
            patches = jnp.concatenate(pieces, axis=0).astype(BF16)
            rows = slice(hf * 256, hf * 256 + 256)
            flow[rows, :] = mm(patches, w_embed[...]).astype(BF16).astype(F32)
            swin_rows(flow, qkv, att, hf * 4, 4, lambda n: bias0[n], w_qkv, w_proj, w_up, w_down, norm_gains, 0)
            first[rows, :] = flow[rows, :].astype(BF16)
            if hf == 0:
                send(first.at[pl.ds(0, 128)], from_right.at[t], (ty, left), 5)
                send(first.at[pl.ds(0, 64)], from_corner.at[t], (above, left), 6)
            for wk in (2 * hf, 2 * hf + 1):
                send(first.at[pl.ds(wk * 128, 64)], from_below.at[t, wk], (above, tx), 7 + wk)
            for w in range(hf * 4, hf * 4 + 4):
                wk, wi = w // 2, w % 2
                for p in range(8):
                    row = w * 64 + p * 8
                    padded[wi * 8 + p, wk * 8 : wk * 8 + 8, :] = first[row : row + 8, :].astype(F32)

        def bias1(n):
            wi, wk = n // 4, n % 4

            def label(x):
                return 3 * region(ty * ROWS + wi * 8 + x // 8, sr) + region(tx * COLS + wk * 8 + x % 8, sc_)

            return jnp.where(label(key) == label(query), 0.0, -1e30)

        def shifted(start, count):
            swin_rows(flow, qkv, att, start, count, bias1, w_qkv, w_proj, w_up, w_down, norm_gains, 1)
            rows = slice(start * 64, (start + count) * 64)
            est = mm(flow[rows, :].astype(BF16), w_unembed[...])
            sa[start : start + count] = est.astype(BF16).reshape(count, 64, PIX)
            return est

        def place(est, start, count):
            for n in range(start, start + count):
                wi, wk = n // 4, n % 4
                for p in range(8):
                    row = (n - start) * 64 + p * 8
                    around[8 + wi * 8 + p, 8 + wk * 8 : 16 + wk * 8, :] = est[row : row + 8, :]

        for p in range(8):
            rolled = pltpu.roll(padded[p + sr, 0:COLS, :], COLS - sc_, 0)
            for wk in range(3):
                row = wk * 64 + p * 8
                flow[row : row + 8, :] = rolled[wk * 8 : wk * 8 + 8, :]
        place(shifted(0, 3), 0, 3)
        for copy in sends:
            copy.wait()
        sends.clear()
        for p in range(8):
            for wk in range(4):
                padded[16 + p, wk * 8 : wk * 8 + 8, :] = from_below[t, wk, p * 8 : p * 8 + 8, :].astype(F32)
            for wi in range(2):
                at = wi * 64 + p * 8
                padded[wi * 8 + p, 32:40, :] = from_right[t, at : at + 8, :].astype(F32)
            padded[16 + p, 32:40, :] = from_corner[t, p * 8 : p * 8 + 8, :].astype(F32)
        for i in range(ROWS):
            rolled = pltpu.roll(padded[i + sr], COLS + 8 - sc_, 0)
            for wk in range(3 if i < 8 else 0, 4):
                row = ((i // 8 * 4 + wk) * 8 + i % 8) * 8
                flow[row : row + 8, :] = rolled[wk * 8 : wk * 8 + 8, :]
        est = shifted(3, 5)
        send(sa.at[pl.ds(4, 4)], to_below.at[t], (below, tx), 11)
        send(sa.at[3], to_right.at[t, 0], (ty, right), 12)
        send(sa.at[7], to_right.at[t, 1], (ty, right), 13)
        send(sa.at[7], to_corner.at[t], (below, right), 14)
        place(est, 3, 5)
        if t + 1 < STEPS:

            def add_noise(row, lane, piece):
                half[row : row + 8, lane : lane + 128] = half[row : row + 8, lane : lane + 128] + SIGMAS[t + 1] * piece

            need("noise")
            pixels_to_patches(lambda r, c: noise[r : r + 8, c : c + 128], add_noise)
        for copy in sends:
            copy.wait()
        for p in range(8):
            for wi in range(2):
                around[8 + wi * 8 + p, 0:8, :] = to_right[t, wi, p * 8 : p * 8 + 8, :].astype(F32)
            for wk in range(4):
                around[p, 8 + wk * 8 : 16 + wk * 8, :] = to_below[t, wk, p * 8 : p * 8 + 8, :].astype(F32)
            around[p, 0:8, :] = to_corner[t, p * 8 : p * 8 + 8, :].astype(F32)
        for i in range(ROWS):
            rows = slice(i * COLS, i * COLS + COLS)
            piece = pltpu.roll(around[8 + i - sr], COLS + sc_, 0)[:COLS]
            state[rows, :] = half[rows, :] - SIGMAS[t] * piece
        if t + 1 == STEPS:

            def give(row, lane, piece):
                out[row : row + 8, lane : lane + 128] = piece

            patches_to_pixels(lambda r, c: state[r : r + 8, c : c + 128], give)


def per_device(consts, image, noise, offsets, key_mask, gains, observed, vis_weight, w_embed, w_qkv, w_proj, w_up, w_down, w_unembed, norm_gains):
    w1, w4, tw1, f1, f2, w2, w3, tw2, tw3, m2, m3 = consts
    arrays = dict(
        image=image, key_mask=key_mask, w1=w1, tw1=tw1, f1=f1, gains=gains, observed=observed, weight=vis_weight,
        w2=w2, w3=w3, tw2=tw2, tw3=tw3, m2=m2, m3=m3, f2=f2, w4=w4, norm_gains=norm_gains, w_embed=w_embed,
        w_qkv=w_qkv, w_proj=w_proj, w_up=w_up, w_down=w_down, w_unembed=w_unembed, noise=noise,
    )
    moved = [arrays[name] for name in NAMES]
    V = pltpu.VMEM
    held = [V(x.shape[1:] if name == "noise" else x.shape, x.dtype) for name, x in zip(NAMES, moved)]
    scratch = held + [
        V((TOKENS, PIX), F32),
        V((TOKENS, PIX), F32),
        V((NTX, 64, PIX), BF16),
        V((STEPS, NTX, 64, PIX), BF16),
        V((DEV, 16, 128), BF16),
        V((STEPS, DEV, 16, 128), BF16),
        V((DEV, 16, 128), BF16),
        V((STEPS, DEV, 16, 128), BF16),
        V((2, NTX, 32, PIX), BF16),
        V((STEPS, 2, NTX, 32, PIX), BF16),
        V((DEV * 16, 128), F32),
        V((1024, 128), F32),
        V((256, 1024), F32),
        V((3, 64, 2048), F32),
        V((TOKENS, D), F32),
        V((TOKENS, 3 * D), BF16),
        V((TOKENS, D), BF16),
        V((TOKENS, D), BF16),
        V((ROWS + 8, COLS + 8, D), F32),
        V((ROWS + 8, COLS + 8, PIX), F32),
        V((STEPS, 128, D), BF16),
        V((STEPS, 4, 64, D), BF16),
        V((STEPS, 64, D), BF16),
        V((STEPS, 2, 64, PIX), BF16),
        V((STEPS, 4, 64, PIX), BF16),
        V((STEPS, 64, PIX), BF16),
        V((8, 128, 64), F32),
        pltpu.SemaphoreType.DMA((len(NAMES),)),
        pltpu.SemaphoreType.DMA((STEPS * 16,)),
        pltpu.SemaphoreType.DMA((STEPS * 16,)),
    ]
    stepped = pl.pallas_call(
        kernel,
        out_shape=jax.ShapeDtypeStruct(image.shape, F32),
        in_specs=[pl.BlockSpec(memory_space=pltpu.SMEM)] + [pl.BlockSpec(memory_space=pl.ANY)] * len(NAMES),
        out_specs=pl.BlockSpec(memory_space=pltpu.VMEM),
        scratch_shapes=scratch,
        compiler_params=pltpu.CompilerParams(collective_id=0, has_side_effects=True, vmem_limit_bytes=60 * 2**20),
    )(offsets, *moved)
    return stepped + SIGMAS[STEPS] * noise[STEPS - 1]


def solution(mesh):
    consts = tables()
    in_specs = (
        P("ty", "tx"),
        P(None, "ty", "tx"),
        P(),
        P("ty", "tx"),
        P(None, ("ty", "tx"), None),
        P(None, ("ty", "tx"), None),
        P(("ty", "tx"), None),
        P(),
        P(),
        P(),
        P(),
        P(),
        P(),
        P(),
    )
    consts_specs = (P(),) * len(consts)
    mapped = jax.shard_map(
        lambda c, *args: per_device(c, *args),
        mesh=mesh,
        in_specs=(consts_specs,) + in_specs,
        out_specs=P("ty", "tx"),
        check_vma=False,
    )
    return lambda *args: mapped(tuple(jnp.asarray(c) for c in consts), *args)
```

```python
import functools
import math

import jax
import jax.numpy as jnp
import numpy as np
from jax import lax
from jax.experimental import pallas as pl
from jax.experimental.pallas import tpu as pltpu
from jax.sharding import PartitionSpec as P

N = 4096
WIN = 8
D = 512
HEADS = 8
FF = 2048
STEPS = 2
NTY = 16
NTX = 8
DEV = NTY * NTX
ROWS = 16
COLS = 32
TOKENS = ROWS * COLS
PIX = 256
SIDE = 256
SIGMAS = (0.8, 0.5, 0.3)
STEP_SIZES = (0.9, 0.7)
EPSILON = 1e-05
MESH = pl.DeviceIdType.MESH
F32 = jnp.float32
BF16 = jnp.bfloat16


def tables():
    k1 = np.array([32 * t + 16 * h + m for h in range(2) for t in range(8) for m in range(16)])
    k = np.arange(256)
    ang = 2 * np.pi * ((k1[:, None] * k[None, :]) % 256) / 256
    w1 = np.concatenate([np.cos(ang), -np.sin(ang)], axis=0)
    w4 = w1.T
    b = np.tile(np.arange(16), 16)
    ang = 2 * np.pi * (k1[:, None] * b[None, :]) / 4096
    tw1 = np.stack([np.cos(ang), np.sin(ang)])
    eye = np.eye(32)
    b16 = np.arange(16)
    ang = 2 * np.pi * ((b16[:, None] * b16[None, :]) % 16) / 16
    wr, wi = np.cos(ang), -np.sin(ang)
    core = np.zeros((2, 16, 16, 2))
    core[0, :, :, 0], core[0, :, :, 1] = wr, wi
    core[1, :, :, 0], core[1, :, :, 1] = -wi, wr
    core = core.reshape(2, 16, 8, 2, 2)
    f1 = np.einsum("cbpld,xy->cxbpdly", core, eye).reshape(1024, 1024)
    wi = -wi
    core = np.zeros((16, 2, 2, 16))
    core[:, 0, 0], core[:, 0, 1] = wr, wi
    core[:, 1, 0], core[:, 1, 1] = -wi, wr
    core = core.reshape(8, 2, 2, 2, 16)
    f2 = np.einsum("plcdb,xy->pclxdyb", core, eye).reshape(1024, 1024)
    u = np.arange(128)
    ang = 2 * np.pi * ((u[:, None] * u[None, :]) % 128) / 128
    w2 = np.concatenate([np.cos(ang), -np.sin(ang)], axis=1)
    w3 = np.concatenate([np.cos(ang), np.sin(ang)], axis=1)
    rho = np.arange(32)
    ang = 2 * np.pi * (rho[:, None] * u[None, :]) / 4096
    c, s = np.cos(ang), np.sin(ang)
    tw2c = np.concatenate([c, c, c, c], axis=0).T
    tw2s = np.concatenate([s, s, -s, -s], axis=0).T
    tw2 = np.stack([tw2c, tw2s])
    tw3 = np.stack([np.concatenate([c, c]), np.concatenate([s, s])]) / N
    ang = 2 * np.pi * ((rho[:, None] * rho[None, :]) % 32) / 32
    wr, wi = np.cos(ang), -np.sin(ang)
    eye2 = np.eye(2)

    def block(wr, wi):
        return np.block([[np.kron(eye2, wr), np.kron(eye2, -wi)], [np.kron(eye2, wi), np.kron(eye2, wr)]])

    m2 = block(wr, wi)
    m3 = block(wr, -wi)
    half = lambda x: np.asarray(x, np.float32).astype(BF16)
    full = lambda x: np.asarray(x, np.float32)
    return (half(w1), half(w4), full(tw1), half(f1), half(f2), half(w2), half(w3), full(tw2), full(tw3), half(m2), half(m3))


def mm(a, b):
    return jnp.dot(a, b, preferred_element_type=F32)


def nt(a, b):
    return lax.dot_general(a, b, (((1,), (1,)), ((), ())), preferred_element_type=F32)


def swap_blocks(x):
    sub = lax.broadcasted_iota(jnp.int32, x.shape, 1)
    lane = lax.broadcasted_iota(jnp.int32, x.shape, 2) // 16
    for d in (4, 2, 1):
        bs = (sub // d) % 2
        bl = (lane // d) % 2
        after = pltpu.roll(pltpu.roll(x, 8 - d, 1), 16 * d, 2)
        if d == 4:
            x = jnp.where(bs == bl, x, after)
        else:
            before = pltpu.roll(pltpu.roll(x, d, 1), 128 - 16 * d, 2)
            x = jnp.where(bs == bl, x, jnp.where(bs == 0, after, before))
    return x


def pixels_to_patches(read, write):
    for i in range(ROWS):
        pieces = [read(i * 16 + ah * 8, kh * 128) for kh in range(4) for ah in range(2)]
        out = swap_blocks(jnp.stack(pieces))
        for kh in range(4):
            for ah in range(2):
                write(i * COLS + kh * 8, ah * 128, out[kh * 2 + ah])


def patches_to_pixels(read, write):
    for i in range(ROWS):
        pieces = [read(i * COLS + kh * 8, ah * 128) for kh in range(4) for ah in range(2)]
        out = swap_blocks(jnp.stack(pieces))
        for kh in range(4):
            for ah in range(2):
                write(i * 16 + ah * 8, kh * 128, out[kh * 2 + ah])


def coords(d):
    return (d // NTX, lax.rem(d, NTX))


def begin(mine, count, peer, src, dst, send_sem, recv_sem):
    def send(o, carry):
        t = lax.rem(mine + o, count)
        pltpu.make_async_remote_copy(
            src.at[t], dst.at[mine], send_sem, recv_sem, device_id=peer(t), device_id_type=MESH
        ).start()
        return carry

    lax.fori_loop(1, count, send, 0)
    dst[mine] = src[mine]

    def finish():
        rest = pltpu.make_async_remote_copy(
            src.at[pl.ds(0, count - 1)],
            dst.at[pl.ds(0, count - 1)],
            send_sem,
            recv_sem,
            device_id=peer(lax.rem(mine + 1, count)),
            device_id_type=MESH,
        )
        rest.wait_send()
        rest.wait_recv()

    return finish


def exchange(*args):
    begin(*args)()


def layer_norm(values, gain):
    centre = jnp.mean(values, axis=-1, keepdims=True)
    shifted = values - centre
    spread = jnp.mean(shifted * shifted, axis=-1, keepdims=True)
    return shifted * lax.rsqrt(spread + EPSILON) * gain


def gelu(v):
    return 0.5 * v * (1.0 + jnp.tanh(math.sqrt(2.0 / math.pi) * (v + 0.044715 * (v * v * v))))


def swin_rows(flow, qkv, att, start, count, bias_of, w_qkv, w_proj, w_up, w_down, gains, j):
    rows = slice(start * 64, (start + count) * 64)
    normed = layer_norm(flow[rows, :], gains[j, 0:1, :]).astype(BF16)
    qkv[rows, :] = mm(normed, w_qkv[j]).astype(BF16)
    lane = lax.broadcasted_iota(jnp.int32, (1, 128), 1)
    low = lane < 64
    pick_low = jnp.where(low, 0.125, 0.0).astype(BF16)
    pick_high = jnp.where(low, 0.0, 0.125).astype(BF16)
    for n in range(start, start + count):
        at = slice(n * 64, n * 64 + 64)
        bias = bias_of(n)
        for pair in range(4):
            cols = slice(pair * 128, pair * 128 + 128)
            q = qkv[at, cols]
            k = qkv[at, D + pair * 128 : D + pair * 128 + 128]
            v = qkv[at, 2 * D + pair * 128 : 2 * D + pair * 128 + 128]
            both = jnp.concatenate([q * pick_low, q * pick_high], axis=0)
            scores = nt(both, k) + bias
            weights = jnp.exp(scores - jnp.max(scores, axis=1, keepdims=True))
            probs = weights * (1.0 / jnp.sum(weights, axis=1, keepdims=True))
            mixed = mm(probs.astype(BF16), v)
            att[at, cols] = jnp.where(low, mixed[:64], mixed[64:]).astype(BF16)
    after = flow[rows, :] + mm(att[rows, :], w_proj[j])
    normed = layer_norm(after, gains[j, 1:2, :]).astype(BF16)
    for c in range(0, FF, 512):
        hidden = gelu(mm(normed, w_up[j, :, c : c + 512])).astype(BF16)
        after = after + mm(hidden, w_down[j, c : c + 512, :])
    flow[rows, :] = after


def region(index, shift):
    return jnp.where(index < SIDE - WIN, 0, jnp.where(index < SIDE - shift, 1, 2))


NAMES = (
    "image", "key_mask", "w1", "tw1", "f1", "gains", "observed", "weight", "w2", "w3", "tw2", "tw3", "m2", "m3", "f2", "w4",
    "norm_gains", "w_embed", "w_qkv", "w_proj", "w_up", "w_down", "w_unembed", "noise",
)


def kernel(offsets, *refs):
    count = len(NAMES)
    sources = refs[:count]
    out = refs[count]
    held = refs[count + 1 : 2 * count + 1]
    (
        image, key_mask, w1, tw1, f1, gains, observed, weight, w2, w3, tw2, tw3, m2, m3, f2, w4,
        norm_gains, w_embed, w_qkv, w_proj, w_up, w_down, w_unembed, noise,
    ) = held
    (
        state, half, sa, ra, sb, rb, sc, rc, sd, rd, xf, xg, abr, flow, qkv, att, first, padded, around,
        from_right, from_below, from_corner, to_right, to_below, to_corner, bias0, vst, load_sem, send_sem, recv_sem, wide_sem, arrived,
    ) = refs[2 * count + 1 :]
    ty = lax.axis_index("ty")
    tx = lax.axis_index("tx")
    me = ty * NTX + tx
    barrier = pltpu.get_barrier_semaphore()

    for o in range(1, NTX):
        pl.semaphore_signal(barrier, inc=1, device_id=(ty, lax.rem(tx + o, NTX)), device_id_type=MESH)
    for o in range(1, NTY):
        pl.semaphore_signal(barrier, inc=1, device_id=(lax.rem(ty + o, NTY), tx), device_id_type=MESH)
    loads = {}
    for n, name in enumerate(NAMES):
        source = sources[n].at[0] if name == "noise" else sources[n]
        loads[name] = pltpu.make_async_copy(source, held[n], load_sem.at[n])
        loads[name].start()

    def need(*names):
        for name in names:
            if name in loads:
                loads.pop(name).wait()

    need("image")
    mine = me // 32

    def scatter(prepare, src, dst, send, recv):
        for j in range(4):
            g = lax.rem(mine + j, 4)
            prepare(g)

            def one(o, carry):
                d = g * 32 + lax.rem(lax.rem(me, 32) + o, 32)
                pltpu.make_async_remote_copy(
                    src.at[d], dst.at[me], send, wide_sem.at[recv + mine], device_id=coords(d), device_id_type=MESH
                ).start()
                return carry

            lax.fori_loop(1 if j == 0 else 0, 32, one, 0)
        dst[me] = src[me]

    def gather(take, src, dst, send, recv):
        def blocks(count, g):
            return pltpu.make_async_remote_copy(
                src.at[pl.ds(0, count)],
                dst.at[pl.ds(0, count)],
                send,
                wide_sem.at[recv + g],
                device_id=coords(lax.rem(me + 1, DEV)),
                device_id_type=MESH,
            )

        for j in range(4):
            g = lax.rem(mine + 4 - j, 4)
            blocks(31 if j == 0 else 32, g).wait_recv()
            take(g)
        blocks(DEV - 1, 0).wait_send()

    def put_state(row, lane, piece):
        state[row : row + 8, lane : lane + 128] = piece

    pixels_to_patches(lambda r, c: image[r : r + 8, c : c + 128], put_state)
    lane = lax.broadcasted_iota(jnp.int32, (128, 128), 1)
    low = (lane // 32) % 2 == 0
    sign = jnp.where(lane < 64, -1.0, 1.0)
    right = lax.rem(tx + 1, NTX)
    left = lax.rem(tx + NTX - 1, NTX)
    below = lax.rem(ty + 1, NTY)
    above = lax.rem(ty + NTY - 1, NTY)

    need("key_mask")
    key = lax.broadcasted_iota(jnp.int32, (1, 64), 1)
    query = lax.broadcasted_iota(jnp.int32, (128, 1), 0) % 64
    spot = lax.broadcasted_iota(jnp.int32, (64, 1), 0)
    mask_lane = lax.broadcasted_iota(jnp.int32, (64, COLS), 1)
    for w in range(8):
        wk, wi = w // 2, w % 2
        lines = [jnp.broadcast_to(key_mask[wi * 8 + p : wi * 8 + p + 1, :], (8, COLS)) for p in range(8)]
        lines = jnp.concatenate(lines, axis=0)
        kept = jnp.sum(jnp.where(mask_lane == wk * 8 + spot % 8, lines, 0).astype(F32), axis=1, keepdims=True)
        kept = jnp.sum(jnp.where(spot == key, kept, 0.0), axis=0, keepdims=True)
        bias0[w] = jnp.where((kept == 1.0) | (key == query), 0.0, -1e30)

    for t in range(STEPS):
        base = t * 16

        sa[...] = state[...].astype(BF16).reshape(NTX, 64, PIX)
        if t == 0:
            pl.semaphore_wait(barrier, NTX + NTY - 2)
            for o in range(1, NTY):
                pl.semaphore_signal(arrived, inc=1, device_id=(lax.rem(ty + o, NTY), tx), device_id_type=MESH)
        exchange(tx, NTX, lambda n: (ty, n), sa, ra.at[t], send_sem.at[base], recv_sem.at[base])
        got = ra[t]
        slab = jnp.concatenate([got[:, :32, :].reshape(256, PIX), got[:, 32:, :].reshape(256, PIX)], axis=1)
        need("w1", "tw1")
        cos1 = jnp.concatenate([tw1[0], tw1[0]], axis=1)
        sin1 = jnp.concatenate([tw1[1], tw1[1]], axis=1)
        part = mm(w1[...], slab)
        pr, pi = part[:256], part[256:]
        part = jnp.concatenate([pr * cos1 + pi * sin1, pi * cos1 - pr * sin1], axis=1).astype(BF16)
        need("f1")
        if t == 0:
            pl.semaphore_wait(arrived, NTY - 1)

        def leave_rows(g):
            out = mm(part, f1[:, pl.ds(pl.multiple_of(g * 256, 256), 256)])
            for e in range(2):
                a0 = out[0:128, e * 128 : e * 128 + 128]
                a1 = out[128:256, e * 128 : e * 128 + 128]
                at = g * 32 + e * 16
                sb[pl.ds(at, 8)] = jnp.where(low, a0, pltpu.roll(a1, 32, 1)).astype(BF16).reshape(8, 16, 128)
                sb[pl.ds(at + 8, 8)] = jnp.where(low, pltpu.roll(a0, 96, 1), a1).astype(BF16).reshape(8, 16, 128)

        scatter(leave_rows, sb, rb.at[t], send_sem.at[base + 1], t * 8)

        if t == 0:
            need("gains", "observed", "weight", "w2", "w3", "tw2", "tw3", "m2", "m3")
            for q in range(4):
                rows = slice(q * 8, q * 8 + 8)
                for v in range(32):
                    cols = slice(v * 128, v * 128 + 128)
                    gr, gi = gains[0, rows, cols], gains[1, rows, cols]
                    zr, zi = observed[0, rows, cols], observed[1, rows, cols]
                    wt = weight[rows, cols]
                    at = slice((q * 32 + v) * 8, (q * 32 + v) * 8 + 8)
                    xf[at, :] = (wt * (gr * gr + gi * gi)) * (1.0 / N)
                    xf[1024 + at.start : 1024 + at.stop, :] = wt * (gr * zr + gi * zi)
                    xg[at, :] = wt * (gr * zi - gi * zr)
            for q in range(4):
                h, mh = q // 2, q % 2
                for ml in range(8):
                    cols = slice((mh * 8 + ml) * 128, (mh * 8 + ml) * 128 + 128)
                    abr[0, h * 32 : h * 32 + 32, cols] = xf[pl.ds(q * 256 + ml, 32, stride=8), :]
                    abr[1, h * 32 : h * 32 + 32, cols] = xf[pl.ds(1024 + q * 256 + ml, 32, stride=8), :]
                    abr[2, h * 32 : h * 32 + 32, cols] = xg[pl.ds(q * 256 + ml, 32, stride=8), :]

        def take_rows(g):
            at = pl.multiple_of(g * 512, 512)
            xf[pl.ds(at, 512), :] = rb[t, pl.ds(g * 32, 32)].reshape(512, 128).astype(F32)

        gather(take_rows, sb, rb.at[t], send_sem.at[base + 1], t * 8)
        for m4 in range(0, 16, 4):
            xs = [xf[pl.ds(m4 + n, DEV, stride=16), :] for n in range(4)]
            turned = [pltpu.roll(x, 64, 1) * sign for x in xs]
            both = jnp.concatenate([jnp.concatenate(xs, axis=1), jnp.concatenate(turned, axis=1)], axis=0).astype(BF16)
            y = mm(w2[...], both)
            ys = [y[:, n * 128 : n * 128 + 128] for n in range(4)]
            ys = [x * tw2[0] + pltpu.roll(x, 64, 1) * tw2[1] for x in ys]
            z = nt(m2[...], jnp.concatenate(ys, axis=0).astype(BF16))
            cols = slice(m4 * 128, m4 * 128 + 512)
            fac = abr[0, :, cols]
            back = jnp.concatenate([fac * z[:64] - abr[1, :, cols], fac * z[64:] - abr[2, :, cols]], axis=0)
            v = mm(m3[...], back.astype(BF16))
            rows = []
            for n in range(4):
                vr, vi = v[:64, n * 128 : n * 128 + 128], v[64:, n * 128 : n * 128 + 128]
                xr = vr * tw3[0] - vi * tw3[1]
                xi = vi * tw3[0] + vr * tw3[1]
                rows.append(jnp.concatenate([jnp.concatenate([xr, xi], axis=0), jnp.concatenate([-xi, xr], axis=0)], axis=1))
            vst[m4 * 128 : m4 * 128 + 512, :] = jnp.concatenate(rows, axis=0).astype(BF16)

        def leave_cols(g):
            u = nt(w3[pl.ds(pl.multiple_of(g * 32, 32), 32), :], vst[...])
            for m in range(16):
                xg[pl.ds(m, 32, stride=16), :] = u[:, m * 128 : m * 128 + 128]
            sc[pl.ds(g * 32, 32)] = xg[0:512, :].astype(BF16).reshape(32, 16, 128)

        scatter(leave_cols, sc, rc.at[t], send_sem.at[base + 2], t * 8 + 4)
        need("f2", "w4")
        sums = []

        def take_cols(g):
            low_half, high_half = [], []
            for e in range(2):
                at = g * 32 + e * 16
                r0 = rc[t, pl.ds(at, 8)].reshape(128, 128).astype(F32)
                r1 = rc[t, pl.ds(at + 8, 8)].reshape(128, 128).astype(F32)
                low_half.append(jnp.where(low, r0, pltpu.roll(r1, 32, 1)))
                high_half.append(jnp.where(low, pltpu.roll(r0, 96, 1), r1))
            both = jnp.concatenate([jnp.concatenate(low_half, axis=1), jnp.concatenate(high_half, axis=1)], axis=0)
            term = mm(both.astype(BF16), f2[pl.ds(pl.multiple_of(g * 256, 256), 256), :])
            sums.append(sums[-1] + term if sums else term)

        gather(take_cols, sc, rc.at[t], send_sem.at[base + 2], t * 8 + 4)
        part = sums[-1]
        pr, pi = part[:, :512], part[:, 512:]
        part = jnp.concatenate([pr * cos1 - pi * sin1, pi * cos1 + pr * sin1], axis=0)
        part = part.astype(BF16)

        gradient = []
        for hf in range(2):
            for n in range(NTX):
                y = mm(w4[n * 32 + hf * 16 : n * 32 + hf * 16 + 16, :], part).astype(BF16)
                sd[hf, n, 0:16, :] = y[:, :PIX]
                sd[hf, n, 16:32, :] = y[:, PIX:]
            gradient.append(
                begin(tx, NTX, lambda n: (ty, n), sd.at[hf], rd.at[t, hf], send_sem.at[base + 3 + hf], recv_sem.at[base + 3 + hf])
            )

        need("w_embed", "w_qkv", "w_proj", "w_up", "w_down", "w_unembed", "norm_gains")
        sr = offsets[t, 0]
        sc_ = offsets[t, 1]
        sends = []

        def send(src, dst, who, n):
            copy = pltpu.make_async_remote_copy(
                src, dst, send_sem.at[base + n], recv_sem.at[base + n], device_id=who, device_id_type=MESH
            )
            copy.start()
            sends.append(copy)

        for hf in range(2):
            gradient[hf]()
            grad = rd[t, hf].astype(F32)
            pieces = []
            for w in range(hf * 4, hf * 4 + 4):
                wk, wi = w // 2, w % 2
                for p in range(8):
                    i = wi * 8 + p
                    at = i * COLS + wk * 8
                    move = grad[i // 2, (i % 2) * 16 + (wk % 2) * 8 : (i % 2) * 16 + (wk % 2) * 8 + 8, :]
                    piece = state[at : at + 8, :] - STEP_SIZES[t] * move
                    half[at : at + 8, :] = piece
                    pieces.append(piece)
            patches = jnp.concatenate(pieces, axis=0).astype(BF16)
            rows = slice(hf * 256, hf * 256 + 256)
            flow[rows, :] = mm(patches, w_embed[...]).astype(BF16).astype(F32)
            swin_rows(flow, qkv, att, hf * 4, 4, lambda n: bias0[n], w_qkv, w_proj, w_up, w_down, norm_gains, 0)
            first[rows, :] = flow[rows, :].astype(BF16)
            if hf == 0:
                send(first.at[pl.ds(0, 128)], from_right.at[t], (ty, left), 5)
                send(first.at[pl.ds(0, 64)], from_corner.at[t], (above, left), 6)
            for wk in (2 * hf, 2 * hf + 1):
                send(first.at[pl.ds(wk * 128, 64)], from_below.at[t, wk], (above, tx), 7 + wk)
            for w in range(hf * 4, hf * 4 + 4):
                wk, wi = w // 2, w % 2
                for p in range(8):
                    row = w * 64 + p * 8
                    padded[wi * 8 + p, wk * 8 : wk * 8 + 8, :] = first[row : row + 8, :].astype(F32)

        def bias1(n):
            wi, wk = n // 4, n % 4

            def label(x):
                return 3 * region(ty * ROWS + wi * 8 + x // 8, sr) + region(tx * COLS + wk * 8 + x % 8, sc_)

            return jnp.where(label(key) == label(query), 0.0, -1e30)

        def shifted(start, count):
            swin_rows(flow, qkv, att, start, count, bias1, w_qkv, w_proj, w_up, w_down, norm_gains, 1)
            rows = slice(start * 64, (start + count) * 64)
            est = mm(flow[rows, :].astype(BF16), w_unembed[...])
            sa[start : start + count] = est.astype(BF16).reshape(count, 64, PIX)
            return est

        def place(est, start, count):
            for n in range(start, start + count):
                wi, wk = n // 4, n % 4
                for p in range(8):
                    row = (n - start) * 64 + p * 8
                    around[8 + wi * 8 + p, 8 + wk * 8 : 16 + wk * 8, :] = est[row : row + 8, :]

        for p in range(8):
            rolled = pltpu.roll(padded[p + sr, 0:COLS, :], COLS - sc_, 0)
            for wk in range(3):
                row = wk * 64 + p * 8
                flow[row : row + 8, :] = rolled[wk * 8 : wk * 8 + 8, :]
        place(shifted(0, 3), 0, 3)
        for copy in sends:
            copy.wait()
        sends.clear()
        for p in range(8):
            for wk in range(4):
                padded[16 + p, wk * 8 : wk * 8 + 8, :] = from_below[t, wk, p * 8 : p * 8 + 8, :].astype(F32)
            for wi in range(2):
                at = wi * 64 + p * 8
                padded[wi * 8 + p, 32:40, :] = from_right[t, at : at + 8, :].astype(F32)
            padded[16 + p, 32:40, :] = from_corner[t, p * 8 : p * 8 + 8, :].astype(F32)
        for i in range(ROWS):
            rolled = pltpu.roll(padded[i + sr], COLS + 8 - sc_, 0)
            for wk in range(3 if i < 8 else 0, 4):
                row = ((i // 8 * 4 + wk) * 8 + i % 8) * 8
                flow[row : row + 8, :] = rolled[wk * 8 : wk * 8 + 8, :]
        est = shifted(3, 5)
        send(sa.at[pl.ds(4, 4)], to_below.at[t], (below, tx), 11)
        send(sa.at[3], to_right.at[t, 0], (ty, right), 12)
        send(sa.at[7], to_right.at[t, 1], (ty, right), 13)
        send(sa.at[7], to_corner.at[t], (below, right), 14)
        place(est, 3, 5)
        if t + 1 < STEPS:

            def add_noise(row, lane, piece):
                half[row : row + 8, lane : lane + 128] = half[row : row + 8, lane : lane + 128] + SIGMAS[t + 1] * piece

            need("noise")
            pixels_to_patches(lambda r, c: noise[r : r + 8, c : c + 128], add_noise)
        for copy in sends:
            copy.wait()
        for p in range(8):
            for wi in range(2):
                around[8 + wi * 8 + p, 0:8, :] = to_right[t, wi, p * 8 : p * 8 + 8, :].astype(F32)
            for wk in range(4):
                around[p, 8 + wk * 8 : 16 + wk * 8, :] = to_below[t, wk, p * 8 : p * 8 + 8, :].astype(F32)
            around[p, 0:8, :] = to_corner[t, p * 8 : p * 8 + 8, :].astype(F32)
        for i in range(ROWS):
            rows = slice(i * COLS, i * COLS + COLS)
            piece = pltpu.roll(around[8 + i - sr], COLS + sc_, 0)[:COLS]
            state[rows, :] = half[rows, :] - SIGMAS[t] * piece
        if t + 1 == STEPS:

            def give(row, lane, piece):
                out[row : row + 8, lane : lane + 128] = piece

            patches_to_pixels(lambda r, c: state[r : r + 8, c : c + 128], give)


def per_device(consts, image, noise, offsets, key_mask, gains, observed, vis_weight, w_embed, w_qkv, w_proj, w_up, w_down, w_unembed, norm_gains):
    w1, w4, tw1, f1, f2, w2, w3, tw2, tw3, m2, m3 = consts
    arrays = dict(
        image=image, key_mask=key_mask, w1=w1, tw1=tw1, f1=f1, gains=gains, observed=observed, weight=vis_weight,
        w2=w2, w3=w3, tw2=tw2, tw3=tw3, m2=m2, m3=m3, f2=f2, w4=w4, norm_gains=norm_gains, w_embed=w_embed,
        w_qkv=w_qkv, w_proj=w_proj, w_up=w_up, w_down=w_down, w_unembed=w_unembed, noise=noise,
    )
    moved = [arrays[name] for name in NAMES]
    V = pltpu.VMEM
    held = [V(x.shape[1:] if name == "noise" else x.shape, x.dtype) for name, x in zip(NAMES, moved)]
    scratch = held + [
        V((TOKENS, PIX), F32),
        V((TOKENS, PIX), F32),
        V((NTX, 64, PIX), BF16),
        V((STEPS, NTX, 64, PIX), BF16),
        V((DEV, 16, 128), BF16),
        V((STEPS, DEV, 16, 128), BF16),
        V((DEV, 16, 128), BF16),
        V((STEPS, DEV, 16, 128), BF16),
        V((2, NTX, 32, PIX), BF16),
        V((STEPS, 2, NTX, 32, PIX), BF16),
        V((DEV * 16, 128), F32),
        V((1024, 128), F32),
        V((3, 64, 2048), F32),
        V((TOKENS, D), F32),
        V((TOKENS, 3 * D), BF16),
        V((TOKENS, D), BF16),
        V((TOKENS, D), BF16),
        V((ROWS + 8, COLS + 8, D), F32),
        V((ROWS + 8, COLS + 8, PIX), F32),
        V((STEPS, 128, D), BF16),
        V((STEPS, 4, 64, D), BF16),
        V((STEPS, 64, D), BF16),
        V((STEPS, 2, 64, PIX), BF16),
        V((STEPS, 4, 64, PIX), BF16),
        V((STEPS, 64, PIX), BF16),
        V((8, 128, 64), F32),
        V((2048, 256), BF16),
        pltpu.SemaphoreType.DMA((len(NAMES),)),
        pltpu.SemaphoreType.DMA((STEPS * 16,)),
        pltpu.SemaphoreType.DMA((STEPS * 16,)),
        pltpu.SemaphoreType.DMA((STEPS * 2 * 4,)),
        pltpu.SemaphoreType.REGULAR,
    ]
    stepped = pl.pallas_call(
        kernel,
        out_shape=jax.ShapeDtypeStruct(image.shape, F32),
        in_specs=[pl.BlockSpec(memory_space=pltpu.SMEM)] + [pl.BlockSpec(memory_space=pl.ANY)] * len(NAMES),
        out_specs=pl.BlockSpec(memory_space=pltpu.VMEM),
        scratch_shapes=scratch,
        compiler_params=pltpu.CompilerParams(collective_id=0, has_side_effects=True, vmem_limit_bytes=60 * 2**20),
    )(offsets, *moved)
    return stepped + SIGMAS[STEPS] * noise[STEPS - 1]


def solution(mesh):
    consts = tables()
    in_specs = (
        P("ty", "tx"),
        P(None, "ty", "tx"),
        P(),
        P("ty", "tx"),
        P(None, ("ty", "tx"), None),
        P(None, ("ty", "tx"), None),
        P(("ty", "tx"), None),
        P(),
        P(),
        P(),
        P(),
        P(),
        P(),
        P(),
    )
    consts_specs = (P(),) * len(consts)
    mapped = jax.shard_map(
        lambda c, *args: per_device(c, *args),
        mesh=mesh,
        in_specs=(consts_specs,) + in_specs,
        out_specs=P("ty", "tx"),
        check_vma=False,
    )
    return lambda *args: mapped(tuple(jnp.asarray(c) for c in consts), *args)
```

```python
import functools
import math

import jax
import jax.numpy as jnp
import numpy as np
from jax import lax
from jax.experimental import pallas as pl
from jax.experimental.pallas import tpu as pltpu
from jax.sharding import PartitionSpec as P

N = 4096
WIN = 8
D = 512
HEADS = 8
FF = 2048
STEPS = 2
NTY = 16
NTX = 8
DEV = NTY * NTX
ROWS = 16
COLS = 32
TOKENS = ROWS * COLS
PIX = 256
SIDE = 256
SIGMAS = (0.8, 0.5, 0.3)
STEP_SIZES = (0.9, 0.7)
EPSILON = 1e-05
MESH = pl.DeviceIdType.MESH
F32 = jnp.float32
BF16 = jnp.bfloat16


def tables():
    k1 = np.array([32 * t + 16 * h + m for h in range(2) for t in range(8) for m in range(16)])
    k = np.arange(256)
    ang = 2 * np.pi * ((k1[:, None] * k[None, :]) % 256) / 256
    w1 = np.concatenate([np.cos(ang), -np.sin(ang)], axis=0)
    w4 = w1.T
    b = np.tile(np.arange(16), 16)
    ang = 2 * np.pi * (k1[:, None] * b[None, :]) / 4096
    tw1 = np.stack([np.cos(ang), np.sin(ang)])
    eye = np.eye(32)
    b16 = np.arange(16)
    ang = 2 * np.pi * ((b16[:, None] * b16[None, :]) % 16) / 16
    wr, wi = np.cos(ang), -np.sin(ang)
    core = np.zeros((2, 16, 16, 2))
    core[0, :, :, 0], core[0, :, :, 1] = wr, wi
    core[1, :, :, 0], core[1, :, :, 1] = -wi, wr
    core = core.reshape(2, 16, 8, 2, 2)
    f1 = np.einsum("cbpld,xy->cxbpdly", core, eye).reshape(1024, 1024)
    wi = -wi
    core = np.zeros((16, 2, 2, 16))
    core[:, 0, 0], core[:, 0, 1] = wr, wi
    core[:, 1, 0], core[:, 1, 1] = -wi, wr
    core = core.reshape(8, 2, 2, 2, 16)
    f2 = np.einsum("plcdb,xy->pclxdyb", core, eye).reshape(1024, 1024)
    u = np.arange(128)
    ang = 2 * np.pi * ((u[:, None] * u[None, :]) % 128) / 128
    w2 = np.concatenate([np.cos(ang), -np.sin(ang)], axis=1)
    w3 = np.concatenate([np.cos(ang), np.sin(ang)], axis=1)
    rho = np.arange(32)
    ang = 2 * np.pi * (rho[:, None] * u[None, :]) / 4096
    c, s = np.cos(ang), np.sin(ang)
    tw2c = np.concatenate([c, c, c, c], axis=0).T
    tw2s = np.concatenate([s, s, -s, -s], axis=0).T
    tw2 = np.stack([tw2c, tw2s])
    tw3 = np.stack([np.concatenate([c, c]), np.concatenate([s, s])]) / N
    ang = 2 * np.pi * ((rho[:, None] * rho[None, :]) % 32) / 32
    wr, wi = np.cos(ang), -np.sin(ang)
    eye2 = np.eye(2)

    def block(wr, wi):
        return np.block([[np.kron(eye2, wr), np.kron(eye2, -wi)], [np.kron(eye2, wi), np.kron(eye2, wr)]])

    m2 = block(wr, wi)
    m3 = block(wr, -wi)
    ang = 2 * np.pi * (u[:, None] * np.arange(8)[None, :]) / 256
    ph = np.stack([np.cos(ang), np.sin(ang)])
    half = lambda x: np.asarray(x, np.float32).astype(BF16)
    full = lambda x: np.asarray(x, np.float32)
    return (half(w1), half(w4), full(tw1), half(f1), half(f2), half(w2), half(w3), full(tw2), full(tw3), half(m2), half(m3), full(ph))


def mm(a, b):
    return jnp.dot(a, b, preferred_element_type=F32)


def nt(a, b):
    return lax.dot_general(a, b, (((1,), (1,)), ((), ())), preferred_element_type=F32)


def swap_blocks(x):
    sub = lax.broadcasted_iota(jnp.int32, x.shape, 1)
    lane = lax.broadcasted_iota(jnp.int32, x.shape, 2) // 16
    for d in (4, 2, 1):
        bs = (sub // d) % 2
        bl = (lane // d) % 2
        after = pltpu.roll(pltpu.roll(x, 8 - d, 1), 16 * d, 2)
        if d == 4:
            x = jnp.where(bs == bl, x, after)
        else:
            before = pltpu.roll(pltpu.roll(x, d, 1), 128 - 16 * d, 2)
            x = jnp.where(bs == bl, x, jnp.where(bs == 0, after, before))
    return x


def pixels_to_patches(read, write):
    for i in range(ROWS):
        pieces = [read(i * 16 + ah * 8, kh * 128) for kh in range(4) for ah in range(2)]
        out = swap_blocks(jnp.stack(pieces))
        for kh in range(4):
            for ah in range(2):
                write(i * COLS + kh * 8, ah * 128, out[kh * 2 + ah])


def patches_to_pixels(read, write):
    for i in range(ROWS):
        pieces = [read(i * COLS + kh * 8, ah * 128) for kh in range(4) for ah in range(2)]
        out = swap_blocks(jnp.stack(pieces))
        for kh in range(4):
            for ah in range(2):
                write(i * 16 + ah * 8, kh * 128, out[kh * 2 + ah])


def coords(d):
    return (d // NTX, lax.rem(d, NTX))


def begin(mine, count, peer, src, dst, send_sem, recv_sem):
    def send(o, carry):
        t = lax.rem(mine + o, count)
        pltpu.make_async_remote_copy(
            src.at[t], dst.at[mine], send_sem, recv_sem, device_id=peer(t), device_id_type=MESH
        ).start()
        return carry

    lax.fori_loop(1, count, send, 0)
    dst[mine] = src[mine]

    def finish():
        rest = pltpu.make_async_remote_copy(
            src.at[pl.ds(0, count - 1)],
            dst.at[pl.ds(0, count - 1)],
            send_sem,
            recv_sem,
            device_id=peer(lax.rem(mine + 1, count)),
            device_id_type=MESH,
        )
        rest.wait_send()
        rest.wait_recv()

    return finish


def exchange(*args):
    begin(*args)()


def layer_norm(values, gain):
    centre = jnp.mean(values, axis=-1, keepdims=True)
    shifted = values - centre
    spread = jnp.mean(shifted * shifted, axis=-1, keepdims=True)
    return shifted * lax.rsqrt(spread + EPSILON) * gain


def gelu(v):
    return 0.5 * v * (1.0 + jnp.tanh(math.sqrt(2.0 / math.pi) * (v + 0.044715 * (v * v * v))))


def swin_rows(flow, qkv, att, start, count, bias_of, w_qkv, w_proj, w_up, w_down, gains, j):
    rows = slice(start * 64, (start + count) * 64)
    normed = layer_norm(flow[rows, :], gains[j, 0:1, :]).astype(BF16)
    qkv[rows, :] = mm(normed, w_qkv[j]).astype(BF16)
    lane = lax.broadcasted_iota(jnp.int32, (1, 128), 1)
    low = lane < 64
    pick_low = jnp.where(low, 0.125, 0.0).astype(BF16)
    pick_high = jnp.where(low, 0.0, 0.125).astype(BF16)
    for n in range(start, start + count):
        at = slice(n * 64, n * 64 + 64)
        bias = bias_of(n)
        for pair in range(4):
            cols = slice(pair * 128, pair * 128 + 128)
            q = qkv[at, cols]
            k = qkv[at, D + pair * 128 : D + pair * 128 + 128]
            v = qkv[at, 2 * D + pair * 128 : 2 * D + pair * 128 + 128]
            both = jnp.concatenate([q * pick_low, q * pick_high], axis=0)
            scores = nt(both, k) + bias
            weights = jnp.exp(scores - jnp.max(scores, axis=1, keepdims=True))
            probs = weights * (1.0 / jnp.sum(weights, axis=1, keepdims=True))
            mixed = mm(probs.astype(BF16), v)
            att[at, cols] = jnp.where(low, mixed[:64], mixed[64:]).astype(BF16)
    after = flow[rows, :] + mm(att[rows, :], w_proj[j])
    normed = layer_norm(after, gains[j, 1:2, :]).astype(BF16)
    for c in range(0, FF, 512):
        hidden = gelu(mm(normed, w_up[j, :, c : c + 512])).astype(BF16)
        after = after + mm(hidden, w_down[j, c : c + 512, :])
    flow[rows, :] = after


def region(index, shift):
    return jnp.where(index < SIDE - WIN, 0, jnp.where(index < SIDE - shift, 1, 2))


NAMES = (
    "image", "key_mask", "w1", "tw1", "f1", "gains", "observed", "weight", "w2", "w3", "tw2", "tw3", "m2", "m3", "f2", "w4", "ph",
    "norm_gains", "w_embed", "w_qkv", "w_proj", "w_up", "w_down", "w_unembed", "noise",
)


def kernel(offsets, *refs):
    count = len(NAMES)
    sources = refs[:count]
    out = refs[count]
    held = refs[count + 1 : 2 * count + 1]
    (
        image, key_mask, w1, tw1, f1, gains, observed, weight, w2, w3, tw2, tw3, m2, m3, f2, w4, ph,
        norm_gains, w_embed, w_qkv, w_proj, w_up, w_down, w_unembed, noise,
    ) = held
    (
        state, half, sa, ra, sb, rb, sc, rc, sd, rd, xf, xg, abr, flow, qkv, att, first, padded, around,
        from_right, from_below, from_corner, to_right, to_below, to_corner, bias0, vst, eb, hb, hr, hpad, hn_below, hn_right, hn_corner, load_sem, send_sem, recv_sem, wide_sem, arrived,
    ) = refs[2 * count + 1 :]
    ty = lax.axis_index("ty")
    tx = lax.axis_index("tx")
    me = ty * NTX + tx
    barrier = pltpu.get_barrier_semaphore()

    for o in range(1, NTX):
        pl.semaphore_signal(barrier, inc=1, device_id=(ty, lax.rem(tx + o, NTX)), device_id_type=MESH)
    for o in range(1, NTY):
        pl.semaphore_signal(barrier, inc=1, device_id=(lax.rem(ty + o, NTY), tx), device_id_type=MESH)
    loads = {}
    for n, name in enumerate(NAMES):
        source = sources[n].at[0] if name == "noise" else sources[n]
        loads[name] = pltpu.make_async_copy(source, held[n], load_sem.at[n])
        loads[name].start()

    def need(*names):
        for name in names:
            if name in loads:
                loads.pop(name).wait()

    need("image")
    mine = me // 32

    def scatter(prepare, src, dst, send, recv):
        for j in range(4):
            g = lax.rem(mine + j, 4)
            prepare(g)

            def one(o, carry):
                d = g * 32 + lax.rem(lax.rem(me, 32) + o, 32)
                pltpu.make_async_remote_copy(
                    src.at[d], dst.at[me], send, wide_sem.at[recv + mine], device_id=coords(d), device_id_type=MESH
                ).start()
                return carry

            lax.fori_loop(1 if j == 0 else 0, 32, one, 0)
        dst[me] = src[me]

    def gather(take, src, dst, send, recv):
        def blocks(count, g):
            return pltpu.make_async_remote_copy(
                src.at[pl.ds(0, count)],
                dst.at[pl.ds(0, count)],
                send,
                wide_sem.at[recv + g],
                device_id=coords(lax.rem(me + 1, DEV)),
                device_id_type=MESH,
            )

        for j in range(4):
            g = lax.rem(mine + 4 - j, 4)
            blocks(31 if j == 0 else 32, g).wait_recv()
            take(g)
        blocks(DEV - 1, 0).wait_send()

    def put_state(row, lane, piece):
        state[row : row + 8, lane : lane + 128] = piece

    pixels_to_patches(lambda r, c: image[r : r + 8, c : c + 128], put_state)
    lane = lax.broadcasted_iota(jnp.int32, (128, 128), 1)
    low = (lane // 32) % 2 == 0
    sign = jnp.where(lane < 64, -1.0, 1.0)
    right = lax.rem(tx + 1, NTX)
    left = lax.rem(tx + NTX - 1, NTX)
    below = lax.rem(ty + 1, NTY)
    above = lax.rem(ty + NTY - 1, NTY)

    need("key_mask")
    key = lax.broadcasted_iota(jnp.int32, (1, 64), 1)
    query = lax.broadcasted_iota(jnp.int32, (128, 1), 0) % 64
    spot = lax.broadcasted_iota(jnp.int32, (64, 1), 0)
    mask_lane = lax.broadcasted_iota(jnp.int32, (64, COLS), 1)
    for w in range(8):
        wk, wi = w // 2, w % 2
        lines = [jnp.broadcast_to(key_mask[wi * 8 + p : wi * 8 + p + 1, :], (8, COLS)) for p in range(8)]
        lines = jnp.concatenate(lines, axis=0)
        kept = jnp.sum(jnp.where(mask_lane == wk * 8 + spot % 8, lines, 0).astype(F32), axis=1, keepdims=True)
        kept = jnp.sum(jnp.where(spot == key, kept, 0.0), axis=0, keepdims=True)
        bias0[w] = jnp.where((kept == 1.0) | (key == query), 0.0, -1e30)

    returning = []

    def roll_back(t):
        for copy in returning[t]:
            copy.wait()
        for p in range(8):
            for wi in range(2):
                around[8 + wi * 8 + p, 0:8, :] = to_right[t, wi, p * 8 : p * 8 + 8, :].astype(F32)
            for wk in range(4):
                around[p, 8 + wk * 8 : 16 + wk * 8, :] = to_below[t, wk, p * 8 : p * 8 + 8, :].astype(F32)
            around[p, 0:8, :] = to_corner[t, p * 8 : p * 8 + 8, :].astype(F32)
        for i in range(ROWS):
            rows = slice(i * COLS, i * COLS + COLS)
            piece = pltpu.roll(around[8 + i - offsets[t, 0]], COLS + offsets[t, 1], 0)[:COLS]
            state[rows, :] = half[rows, :] - SIGMAS[t] * piece

    for t in range(STEPS):
        base = t * 16

        if t == 0:
            sa[...] = state[...].astype(BF16).reshape(NTX, 64, PIX)
            pl.semaphore_wait(barrier, NTX + NTY - 2)
            for o in range(1, NTY):
                pl.semaphore_signal(arrived, inc=1, device_id=(lax.rem(ty + o, NTY), tx), device_id_type=MESH)
        exchange(tx, NTX, lambda n: (ty, n), sa, ra.at[t], send_sem.at[base], recv_sem.at[base])
        got = ra[t]
        slab = jnp.concatenate([got[:, :32, :].reshape(256, PIX), got[:, 32:, :].reshape(256, PIX)], axis=1)
        cos2, sin2 = tw2.at[0], tw2.at[1]
        if t > 0:
            slab = pltpu.roll(slab.astype(F32), offsets[t - 1, 1], 0).astype(BF16)
            moved = offsets[t - 1, 0]
            eight = lax.broadcasted_iota(jnp.int32, (128, 8), 1)
            pc = jnp.sum(jnp.where(eight == moved, ph[0], 0.0), axis=1, keepdims=True)
            ps = jnp.sum(jnp.where(eight == moved, ph[1], 0.0), axis=1, keepdims=True)
            cos2 = tw2[0] * pc + tw2[1] * sign * ps
            sin2 = tw2[1] * pc - tw2[0] * sign * ps
            odd = lax.broadcasted_iota(jnp.int32, (128, 1), 0) % 2 * (moved % 2)
            flip = 1.0 - 2.0 * odd.astype(F32)
        need("w1", "tw1")
        cos1 = jnp.concatenate([tw1[0], tw1[0]], axis=1)
        sin1 = jnp.concatenate([tw1[1], tw1[1]], axis=1)
        part = mm(w1[...], slab)
        pr, pi = part[:256], part[256:]
        part = jnp.concatenate([pr * cos1 + pi * sin1, pi * cos1 - pr * sin1], axis=1).astype(BF16)
        need("f1")
        if t == 0:
            pl.semaphore_wait(arrived, NTY - 1)

        def leave_rows(g):
            out = mm(part, f1[:, pl.ds(pl.multiple_of(g * 256, 256), 256)])
            for e in range(2):
                a0 = out[0:128, e * 128 : e * 128 + 128]
                a1 = out[128:256, e * 128 : e * 128 + 128]
                at = g * 32 + e * 16
                sb[pl.ds(at, 8)] = jnp.where(low, a0, pltpu.roll(a1, 32, 1)).astype(BF16).reshape(8, 16, 128)
                sb[pl.ds(at + 8, 8)] = jnp.where(low, pltpu.roll(a0, 96, 1), a1).astype(BF16).reshape(8, 16, 128)

        scatter(leave_rows, sb, rb.at[t], send_sem.at[base + 1], t * 8)

        if t == 0:
            need("gains", "observed", "weight", "w2", "w3", "tw2", "tw3", "m2", "m3", "ph")
            for q in range(4):
                rows = slice(q * 8, q * 8 + 8)
                for v in range(32):
                    cols = slice(v * 128, v * 128 + 128)
                    gr, gi = gains[0, rows, cols], gains[1, rows, cols]
                    zr, zi = observed[0, rows, cols], observed[1, rows, cols]
                    wt = weight[rows, cols]
                    at = slice((q * 32 + v) * 8, (q * 32 + v) * 8 + 8)
                    xf[at, :] = (wt * (gr * gr + gi * gi)) * (1.0 / N)
                    xf[1024 + at.start : 1024 + at.stop, :] = wt * (gr * zr + gi * zi)
                    xg[at, :] = wt * (gr * zi - gi * zr)
            for q in range(4):
                h, mh = q // 2, q % 2
                for ml in range(8):
                    cols = slice((mh * 8 + ml) * 128, (mh * 8 + ml) * 128 + 128)
                    abr[0, h * 32 : h * 32 + 32, cols] = xf[pl.ds(q * 256 + ml, 32, stride=8), :]
                    abr[1, h * 32 : h * 32 + 32, cols] = xf[pl.ds(1024 + q * 256 + ml, 32, stride=8), :]
                    abr[2, h * 32 : h * 32 + 32, cols] = xg[pl.ds(q * 256 + ml, 32, stride=8), :]

        def take_rows(g):
            at = pl.multiple_of(g * 512, 512)
            xf[pl.ds(at, 512), :] = rb[t, pl.ds(g * 32, 32)].reshape(512, 128).astype(F32)

        gather(take_rows, sb, rb.at[t], send_sem.at[base + 1], t * 8)
        for m4 in range(0, 16, 4):
            xs = [xf[pl.ds(m4 + n, DEV, stride=16), :] for n in range(4)]
            turned = [pltpu.roll(x, 64, 1) * sign for x in xs]
            both = jnp.concatenate([jnp.concatenate(xs, axis=1), jnp.concatenate(turned, axis=1)], axis=0).astype(BF16)
            y = mm(w2[...], both)
            ys = [y[:, n * 128 : n * 128 + 128] for n in range(4)]
            ys = [x * cos2[...] + pltpu.roll(x, 64, 1) * sin2[...] for x in ys]
            z = nt(m2[...], jnp.concatenate(ys, axis=0).astype(BF16))
            if t > 0:
                z = z * flip
            cols = slice(m4 * 128, m4 * 128 + 512)
            fac = abr[0, :, cols]
            back = jnp.concatenate([fac * z[:64] - abr[1, :, cols], fac * z[64:] - abr[2, :, cols]], axis=0)
            v = mm(m3[...], back.astype(BF16))
            rows = []
            for n in range(4):
                vr, vi = v[:64, n * 128 : n * 128 + 128], v[64:, n * 128 : n * 128 + 128]
                xr = vr * tw3[0] - vi * tw3[1]
                xi = vi * tw3[0] + vr * tw3[1]
                rows.append(jnp.concatenate([jnp.concatenate([xr, xi], axis=0), jnp.concatenate([-xi, xr], axis=0)], axis=1))
            vst[m4 * 128 : m4 * 128 + 512, :] = jnp.concatenate(rows, axis=0).astype(BF16)

        def leave_cols(g):
            u = nt(w3[pl.ds(pl.multiple_of(g * 32, 32), 32), :], vst[...])
            for m in range(16):
                xg[pl.ds(m, 32, stride=16), :] = u[:, m * 128 : m * 128 + 128]
            sc[pl.ds(g * 32, 32)] = xg[0:512, :].astype(BF16).reshape(32, 16, 128)

        scatter(leave_cols, sc, rc.at[t], send_sem.at[base + 2], t * 8 + 4)
        need("f2", "w4")
        sums = []

        def take_cols(g):
            low_half, high_half = [], []
            for e in range(2):
                at = g * 32 + e * 16
                r0 = rc[t, pl.ds(at, 8)].reshape(128, 128).astype(F32)
                r1 = rc[t, pl.ds(at + 8, 8)].reshape(128, 128).astype(F32)
                low_half.append(jnp.where(low, r0, pltpu.roll(r1, 32, 1)))
                high_half.append(jnp.where(low, pltpu.roll(r0, 96, 1), r1))
            both = jnp.concatenate([jnp.concatenate(low_half, axis=1), jnp.concatenate(high_half, axis=1)], axis=0)
            term = mm(both.astype(BF16), f2[pl.ds(pl.multiple_of(g * 256, 256), 256), :])
            sums.append(sums[-1] + term if sums else term)

        gather(take_cols, sc, rc.at[t], send_sem.at[base + 2], t * 8 + 4)
        part = sums[-1]
        pr, pi = part[:, :512], part[:, 512:]
        part = jnp.concatenate([pr * cos1 - pi * sin1, pi * cos1 + pr * sin1], axis=0)
        part = part.astype(BF16)

        gradient = []
        for hf in range(2):
            for n in range(NTX):
                y = mm(w4[n * 32 + hf * 16 : n * 32 + hf * 16 + 16, :], part).astype(BF16)
                sd[hf, n, 0:16, :] = y[:, :PIX]
                sd[hf, n, 16:32, :] = y[:, PIX:]
            gradient.append(
                begin(tx, NTX, lambda n: (ty, n), sd.at[hf], rd.at[t, hf], send_sem.at[base + 3 + hf], recv_sem.at[base + 3 + hf])
            )

        need("w_embed", "w_qkv", "w_proj", "w_up", "w_down", "w_unembed", "norm_gains")
        sr = offsets[t, 0]
        sc_ = offsets[t, 1]
        sends = []

        def send(src, dst, who, n):
            copy = pltpu.make_async_remote_copy(
                src, dst, send_sem.at[base + n], recv_sem.at[base + n], device_id=who, device_id_type=MESH
            )
            copy.start()
            sends.append(copy)

        if t > 0:
            roll_back(t - 1)
        for hf in range(2):
            gradient[hf]()
            grad = rd[t, hf].astype(F32)
            pieces = []
            for w in range(hf * 4, hf * 4 + 4):
                wk, wi = w // 2, w % 2
                for p in range(8):
                    i = wi * 8 + p
                    at = i * COLS + wk * 8
                    move = grad[i // 2, (i % 2) * 16 + (wk % 2) * 8 : (i % 2) * 16 + (wk % 2) * 8 + 8, :]
                    piece = state[at : at + 8, :] - STEP_SIZES[t] * move
                    half[at : at + 8, :] = piece
                    pieces.append(piece)
            patches = jnp.concatenate(pieces, axis=0).astype(BF16)
            rows = slice(hf * 256, hf * 256 + 256)
            flow[rows, :] = mm(patches, w_embed[...]).astype(BF16).astype(F32)
            swin_rows(flow, qkv, att, hf * 4, 4, lambda n: bias0[n], w_qkv, w_proj, w_up, w_down, norm_gains, 0)
            first[rows, :] = flow[rows, :].astype(BF16)
            if hf == 0:
                send(first.at[pl.ds(0, 128)], from_right.at[t], (ty, left), 5)
                send(first.at[pl.ds(0, 64)], from_corner.at[t], (above, left), 6)
            for wk in (2 * hf, 2 * hf + 1):
                send(first.at[pl.ds(wk * 128, 64)], from_below.at[t, wk], (above, tx), 7 + wk)
            for w in range(hf * 4, hf * 4 + 4):
                wk, wi = w // 2, w % 2
                for p in range(8):
                    row = w * 64 + p * 8
                    padded[wi * 8 + p, wk * 8 : wk * 8 + 8, :] = first[row : row + 8, :].astype(F32)

        if t + 1 < STEPS:

            def add_noise(row, lane, piece):
                half[row : row + 8, lane : lane + 128] = half[row : row + 8, lane : lane + 128] + SIGMAS[t + 1] * piece

            need("noise")
            pixels_to_patches(lambda r, c: noise[r : r + 8, c : c + 128], add_noise)
            hb[...] = half[...].astype(BF16)
            hr[...] = jnp.concatenate([half[i * COLS : i * COLS + 8, :] for i in range(ROWS)], axis=0).astype(BF16)
            early = [
                pltpu.make_async_remote_copy(
                    src, dst, send_sem.at[32 + n], recv_sem.at[32 + n], device_id=who, device_id_type=MESH
                )
                for n, (src, dst, who) in enumerate(
                    [
                        (hb.at[pl.ds(0, 256)], hn_below, (above, tx)),
                        (hr, hn_right, (ty, left)),
                        (hr.at[pl.ds(0, 64)], hn_corner, (above, left)),
                    ]
                )
            ]
            for copy in early:
                copy.start()
            for i in range(ROWS):
                hpad[i, 0:COLS, :] = half[i * COLS : i * COLS + COLS, :]

        def bias1(n):
            wi, wk = n // 4, n % 4

            def label(x):
                return 3 * region(ty * ROWS + wi * 8 + x // 8, sr) + region(tx * COLS + wk * 8 + x % 8, sc_)

            return jnp.where(label(key) == label(query), 0.0, -1e30)

        def shifted(start, count):
            swin_rows(flow, qkv, att, start, count, bias1, w_qkv, w_proj, w_up, w_down, norm_gains, 1)
            rows = slice(start * 64, (start + count) * 64)
            est = mm(flow[rows, :].astype(BF16), w_unembed[...])
            eb[start : start + count] = est.astype(BF16).reshape(count, 64, PIX)
            return est

        def place(est, start, count):
            for n in range(start, start + count):
                wi, wk = n // 4, n % 4
                for p in range(8):
                    row = (n - start) * 64 + p * 8
                    around[8 + wi * 8 + p, 8 + wk * 8 : 16 + wk * 8, :] = est[row : row + 8, :]

        for p in range(8):
            rolled = pltpu.roll(padded[p + sr, 0:COLS, :], COLS - sc_, 0)
            for wk in range(3):
                row = wk * 64 + p * 8
                flow[row : row + 8, :] = rolled[wk * 8 : wk * 8 + 8, :]
        place(shifted(0, 3), 0, 3)
        for copy in sends:
            copy.wait()
        sends.clear()
        for p in range(8):
            for wk in range(4):
                padded[16 + p, wk * 8 : wk * 8 + 8, :] = from_below[t, wk, p * 8 : p * 8 + 8, :].astype(F32)
            for wi in range(2):
                at = wi * 64 + p * 8
                padded[wi * 8 + p, 32:40, :] = from_right[t, at : at + 8, :].astype(F32)
            padded[16 + p, 32:40, :] = from_corner[t, p * 8 : p * 8 + 8, :].astype(F32)
        for i in range(ROWS):
            rolled = pltpu.roll(padded[i + sr], COLS + 8 - sc_, 0)
            for wk in range(3 if i < 8 else 0, 4):
                row = ((i // 8 * 4 + wk) * 8 + i % 8) * 8
                flow[row : row + 8, :] = rolled[wk * 8 : wk * 8 + 8, :]
        est = shifted(3, 5)
        back = []
        for n, (src, dst, who) in enumerate(
            [
                (eb.at[pl.ds(4, 4)], to_below.at[t], (below, tx)),
                (eb.at[3], to_right.at[t, 0], (ty, right)),
                (eb.at[7], to_right.at[t, 1], (ty, right)),
                (eb.at[7], to_corner.at[t], (below, right)),
            ]
        ):
            copy = pltpu.make_async_remote_copy(
                src, dst, send_sem.at[base + 11 + n], recv_sem.at[base + 11 + n], device_id=who, device_id_type=MESH
            )
            copy.start()
            back.append(copy)
        returning.append(back)
        place(est, 3, 5)
        if t + 1 < STEPS:
            for copy in early:
                copy.wait()
            for p in range(8):
                hpad[16 + p, 0:COLS, :] = hn_below[p * COLS : p * COLS + COLS, :].astype(F32)
                hpad[16 + p, COLS : COLS + 8, :] = hn_corner[p * 8 : p * 8 + 8, :].astype(F32)
            for i in range(ROWS):
                hpad[i, COLS : COLS + 8, :] = hn_right[i * 8 : i * 8 + 8, :].astype(F32)
            for i in range(ROWS):
                ahead = pltpu.roll(hpad[i + sr], COLS + 8 - sc_, 0)[:COLS]
                ahead = ahead - SIGMAS[t] * around[8 + i, 8 : 8 + COLS, :]
                sa[i // 2, i % 2 * COLS : i % 2 * COLS + COLS, :] = ahead.astype(BF16)
        else:
            roll_back(t)

            def give(row, lane, piece):
                out[row : row + 8, lane : lane + 128] = piece

            patches_to_pixels(lambda r, c: state[r : r + 8, c : c + 128], give)


def per_device(consts, image, noise, offsets, key_mask, gains, observed, vis_weight, w_embed, w_qkv, w_proj, w_up, w_down, w_unembed, norm_gains):
    w1, w4, tw1, f1, f2, w2, w3, tw2, tw3, m2, m3, ph = consts
    arrays = dict(
        image=image, key_mask=key_mask, w1=w1, tw1=tw1, f1=f1, gains=gains, observed=observed, weight=vis_weight,
        w2=w2, w3=w3, tw2=tw2, tw3=tw3, m2=m2, m3=m3, f2=f2, w4=w4, ph=ph, norm_gains=norm_gains, w_embed=w_embed,
        w_qkv=w_qkv, w_proj=w_proj, w_up=w_up, w_down=w_down, w_unembed=w_unembed, noise=noise,
    )
    moved = [arrays[name] for name in NAMES]
    V = pltpu.VMEM
    held = [V(x.shape[1:] if name == "noise" else x.shape, x.dtype) for name, x in zip(NAMES, moved)]
    scratch = held + [
        V((TOKENS, PIX), F32),
        V((TOKENS, PIX), F32),
        V((NTX, 64, PIX), BF16),
        V((STEPS, NTX, 64, PIX), BF16),
        V((DEV, 16, 128), BF16),
        V((STEPS, DEV, 16, 128), BF16),
        V((DEV, 16, 128), BF16),
        V((STEPS, DEV, 16, 128), BF16),
        V((2, NTX, 32, PIX), BF16),
        V((STEPS, 2, NTX, 32, PIX), BF16),
        V((DEV * 16, 128), F32),
        V((1024, 128), F32),
        V((3, 64, 2048), F32),
        V((TOKENS, D), F32),
        V((TOKENS, 3 * D), BF16),
        V((TOKENS, D), BF16),
        V((TOKENS, D), BF16),
        V((ROWS + 8, COLS + 8, D), F32),
        V((ROWS + 8, COLS + 8, PIX), F32),
        V((STEPS, 128, D), BF16),
        V((STEPS, 4, 64, D), BF16),
        V((STEPS, 64, D), BF16),
        V((STEPS, 2, 64, PIX), BF16),
        V((STEPS, 4, 64, PIX), BF16),
        V((STEPS, 64, PIX), BF16),
        V((8, 128, 64), F32),
        V((2048, 256), BF16),
        V((8, 64, PIX), BF16),
        V((TOKENS, PIX), BF16),
        V((128, PIX), BF16),
        V((ROWS + 8, COLS + 8, PIX), F32),
        V((256, PIX), BF16),
        V((128, PIX), BF16),
        V((64, PIX), BF16),
        pltpu.SemaphoreType.DMA((len(NAMES),)),
        pltpu.SemaphoreType.DMA((STEPS * 16 + 3,)),
        pltpu.SemaphoreType.DMA((STEPS * 16 + 3,)),
        pltpu.SemaphoreType.DMA((STEPS * 2 * 4,)),
        pltpu.SemaphoreType.REGULAR,
    ]
    stepped = pl.pallas_call(
        kernel,
        out_shape=jax.ShapeDtypeStruct(image.shape, F32),
        in_specs=[pl.BlockSpec(memory_space=pltpu.SMEM)] + [pl.BlockSpec(memory_space=pl.ANY)] * len(NAMES),
        out_specs=pl.BlockSpec(memory_space=pltpu.VMEM),
        scratch_shapes=scratch,
        compiler_params=pltpu.CompilerParams(collective_id=0, has_side_effects=True, vmem_limit_bytes=60 * 2**20),
    )(offsets, *moved)
    return stepped + SIGMAS[STEPS] * noise[STEPS - 1]


def solution(mesh):
    consts = tables()
    in_specs = (
        P("ty", "tx"),
        P(None, "ty", "tx"),
        P(),
        P("ty", "tx"),
        P(None, ("ty", "tx"), None),
        P(None, ("ty", "tx"), None),
        P(("ty", "tx"), None),
        P(),
        P(),
        P(),
        P(),
        P(),
        P(),
        P(),
    )
    consts_specs = (P(),) * len(consts)
    mapped = jax.shard_map(
        lambda c, *args: per_device(c, *args),
        mesh=mesh,
        in_specs=(consts_specs,) + in_specs,
        out_specs=P("ty", "tx"),
        check_vma=False,
    )
    return lambda *args: mapped(tuple(jnp.asarray(c) for c in consts), *args)
```

```python
import functools
import math

import jax
import jax.numpy as jnp
import numpy as np
from jax import lax
from jax.experimental import pallas as pl
from jax.experimental.pallas import tpu as pltpu
from jax.sharding import PartitionSpec as P

N = 4096
WIN = 8
D = 512
HEADS = 8
FF = 2048
STEPS = 2
NTY = 16
NTX = 8
DEV = NTY * NTX
ROWS = 16
COLS = 32
TOKENS = ROWS * COLS
PIX = 256
SIDE = 256
SIGMAS = (0.8, 0.5, 0.3)
STEP_SIZES = (0.9, 0.7)
EPSILON = 1e-05
MESH = pl.DeviceIdType.MESH
F32 = jnp.float32
BF16 = jnp.bfloat16


def tables():
    k1 = np.array([32 * t + 16 * h + m for h in range(2) for t in range(8) for m in range(16)])
    k = np.arange(256)
    ang = 2 * np.pi * ((k1[:, None] * k[None, :]) % 256) / 256
    w1 = np.concatenate([np.cos(ang), -np.sin(ang)], axis=0)
    w4 = w1.T
    b = np.tile(np.arange(16), 16)
    ang = 2 * np.pi * (k1[:, None] * b[None, :]) / 4096
    tw1 = np.stack([np.cos(ang), np.sin(ang)])
    eye = np.eye(32)
    b16 = np.arange(16)
    ang = 2 * np.pi * ((b16[:, None] * b16[None, :]) % 16) / 16
    wr, wi = np.cos(ang), -np.sin(ang)
    core = np.zeros((2, 16, 16, 2))
    core[0, :, :, 0], core[0, :, :, 1] = wr, wi
    core[1, :, :, 0], core[1, :, :, 1] = -wi, wr
    core = core.reshape(2, 16, 8, 2, 2)
    f1 = np.einsum("cbpld,xy->cxbpdly", core, eye).reshape(1024, 1024)
    wi = -wi
    core = np.zeros((16, 2, 2, 16))
    core[:, 0, 0], core[:, 0, 1] = wr, wi
    core[:, 1, 0], core[:, 1, 1] = -wi, wr
    core = core.reshape(8, 2, 2, 2, 16)
    f2 = np.einsum("plcdb,xy->pclxdyb", core, eye).reshape(1024, 1024)
    u = np.arange(128)
    ang = 2 * np.pi * ((u[:, None] * u[None, :]) % 128) / 128
    w2 = np.concatenate([np.cos(ang), -np.sin(ang)], axis=1)
    w3 = np.concatenate([np.cos(ang), np.sin(ang)], axis=1)
    rho = np.arange(32)
    ang = 2 * np.pi * (rho[:, None] * u[None, :]) / 4096
    c, s = np.cos(ang), np.sin(ang)
    tw2c = np.concatenate([c, c, c, c], axis=0).T
    tw2s = np.concatenate([s, s, -s, -s], axis=0).T
    tw2 = np.stack([tw2c, tw2s])
    tw3 = np.stack([np.concatenate([c, c]), np.concatenate([s, s])]) / N
    ang = 2 * np.pi * ((rho[:, None] * rho[None, :]) % 32) / 32
    wr, wi = np.cos(ang), -np.sin(ang)
    eye2 = np.eye(2)

    def block(wr, wi):
        return np.block([[np.kron(eye2, wr), np.kron(eye2, -wi)], [np.kron(eye2, wi), np.kron(eye2, wr)]])

    m2 = block(wr, wi)
    m3 = block(wr, -wi)
    ang = 2 * np.pi * (u[:, None] * np.arange(8)[None, :]) / 256
    ph = np.stack([np.cos(ang), np.sin(ang)])
    half = lambda x: np.asarray(x, np.float32).astype(BF16)
    full = lambda x: np.asarray(x, np.float32)
    return (half(w1), half(w4), full(tw1), half(f1), half(f2), half(w2), half(w3), full(tw2), full(tw3), half(m2), half(m3), full(ph))


def mm(a, b):
    return jnp.dot(a, b, preferred_element_type=F32)


def nt(a, b):
    return lax.dot_general(a, b, (((1,), (1,)), ((), ())), preferred_element_type=F32)


def swap_blocks(x):
    sub = lax.broadcasted_iota(jnp.int32, x.shape, 1)
    lane = lax.broadcasted_iota(jnp.int32, x.shape, 2) // 16
    for d in (4, 2, 1):
        bs = (sub // d) % 2
        bl = (lane // d) % 2
        after = pltpu.roll(pltpu.roll(x, 8 - d, 1), 16 * d, 2)
        if d == 4:
            x = jnp.where(bs == bl, x, after)
        else:
            before = pltpu.roll(pltpu.roll(x, d, 1), 128 - 16 * d, 2)
            x = jnp.where(bs == bl, x, jnp.where(bs == 0, after, before))
    return x


def pixels_to_patches(read, write):
    for i in range(ROWS):
        pieces = [read(i * 16 + ah * 8, kh * 128) for kh in range(4) for ah in range(2)]
        out = swap_blocks(jnp.stack(pieces))
        for kh in range(4):
            for ah in range(2):
                write(i * COLS + kh * 8, ah * 128, out[kh * 2 + ah])


def patches_to_pixels(read, write):
    for i in range(ROWS):
        pieces = [read(i * COLS + kh * 8, ah * 128) for kh in range(4) for ah in range(2)]
        out = swap_blocks(jnp.stack(pieces))
        for kh in range(4):
            for ah in range(2):
                write(i * 16 + ah * 8, kh * 128, out[kh * 2 + ah])


def coords(d):
    return (d // NTX, lax.rem(d, NTX))


def begin(ty, tx, src, dst, send_sem, recv_sem):
    for o in (1, 7, 2, 6, 3, 5, 4):
        n = lax.rem(tx + o, NTX)
        pltpu.make_async_remote_copy(
            src.at[n], dst.at[tx], send_sem, recv_sem, device_id=(ty, n), device_id_type=MESH
        ).start()
    dst[tx] = src[tx]

    def finish():
        rest = pltpu.make_async_remote_copy(
            src.at[pl.ds(0, NTX - 1)],
            dst.at[pl.ds(0, NTX - 1)],
            send_sem,
            recv_sem,
            device_id=(ty, lax.rem(tx + 1, NTX)),
            device_id_type=MESH,
        )
        rest.wait_send()
        rest.wait_recv()

    return finish


def layer_norm(values, gain):
    centre = jnp.mean(values, axis=-1, keepdims=True)
    shifted = values - centre
    spread = jnp.mean(shifted * shifted, axis=-1, keepdims=True)
    return shifted * lax.rsqrt(spread + EPSILON) * gain


def gelu(v):
    return 0.5 * v * (1.0 + jnp.tanh(math.sqrt(2.0 / math.pi) * (v + 0.044715 * (v * v * v))))


def swin_rows(flow, qkv, att, start, count, bias_of, w_qkv, w_proj, w_up, w_down, gains, j):
    rows = slice(start * 64, (start + count) * 64)
    normed = layer_norm(flow[rows, :], gains[j, 0:1, :]).astype(BF16)
    qkv[rows, :] = mm(normed, w_qkv[j]).astype(BF16)
    lane = lax.broadcasted_iota(jnp.int32, (1, 128), 1)
    low = lane < 64
    pick_low = jnp.where(low, 0.125, 0.0).astype(BF16)
    pick_high = jnp.where(low, 0.0, 0.125).astype(BF16)
    for n in range(start, start + count):
        at = slice(n * 64, n * 64 + 64)
        bias = bias_of(n)
        for pair in range(4):
            cols = slice(pair * 128, pair * 128 + 128)
            q = qkv[at, cols]
            k = qkv[at, D + pair * 128 : D + pair * 128 + 128]
            v = qkv[at, 2 * D + pair * 128 : 2 * D + pair * 128 + 128]
            both = jnp.concatenate([q * pick_low, q * pick_high], axis=0)
            scores = nt(both, k) + bias
            weights = jnp.exp(scores - jnp.max(scores, axis=1, keepdims=True))
            probs = weights * (1.0 / jnp.sum(weights, axis=1, keepdims=True))
            mixed = mm(probs.astype(BF16), v)
            att[at, cols] = jnp.where(low, mixed[:64], mixed[64:]).astype(BF16)
    after = flow[rows, :] + mm(att[rows, :], w_proj[j])
    normed = layer_norm(after, gains[j, 1:2, :]).astype(BF16)
    for c in range(0, FF, 512):
        hidden = gelu(mm(normed, w_up[j, :, c : c + 512])).astype(BF16)
        after = after + mm(hidden, w_down[j, c : c + 512, :])
    flow[rows, :] = after


def region(index, shift):
    return jnp.where(index < SIDE - WIN, 0, jnp.where(index < SIDE - shift, 1, 2))


NAMES = (
    "image", "key_mask", "w1", "tw1", "f1", "gains", "observed", "weight", "w2", "w3", "tw2", "tw3", "m2", "m3", "f2", "w4", "ph",
    "norm_gains", "w_embed", "w_qkv", "w_proj", "w_up", "w_down", "w_unembed", "noise",
)


def kernel(offsets, *refs):
    count = len(NAMES)
    sources = refs[:count]
    out = refs[count]
    held = refs[count + 1 : 2 * count + 1]
    (
        image, key_mask, w1, tw1, f1, gains, observed, weight, w2, w3, tw2, tw3, m2, m3, f2, w4, ph,
        norm_gains, w_embed, w_qkv, w_proj, w_up, w_down, w_unembed, noise,
    ) = held
    (
        state, half, sa, ra, sb, rb, sc, rc, sd, rd, xf, xg, abr, flow, qkv, att, first, padded, around,
        from_right, from_below, from_corner, to_right, to_below, to_corner, bias0, vst, eb, hb, hr, hpad, hn_below, hn_right, hn_corner, load_sem, send_sem, recv_sem, wide_sem, arrived,
    ) = refs[2 * count + 1 :]
    ty = lax.axis_index("ty")
    tx = lax.axis_index("tx")
    me = ty * NTX + tx
    barrier = pltpu.get_barrier_semaphore()

    for o in range(1, NTX):
        pl.semaphore_signal(barrier, inc=1, device_id=(ty, lax.rem(tx + o, NTX)), device_id_type=MESH)
    for o in range(1, NTY):
        pl.semaphore_signal(barrier, inc=1, device_id=(lax.rem(ty + o, NTY), tx), device_id_type=MESH)
    loads = {}
    for n, name in enumerate(NAMES):
        source = sources[n].at[0] if name == "noise" else sources[n]
        loads[name] = pltpu.make_async_copy(source, held[n], load_sem.at[n])
        loads[name].start()

    def need(*names):
        for name in names:
            if name in loads:
                loads.pop(name).wait()

    need("image")
    mine = me // 32

    def scatter(prepare, src, dst, send, recv):
        place = lax.rem(me, 32)

        def leave(g, first, last):
            def one(o, carry):
                d = g * 32 + o
                pltpu.make_async_remote_copy(
                    src.at[d], dst.at[me], send, wide_sem.at[recv + mine], device_id=coords(d), device_id_type=MESH
                ).start()
                return carry

            lax.fori_loop(first, last, one, 0)

        prepare(mine)
        leave(mine, place + 1, 32)
        for j in range(1, 4):
            g = lax.rem(mine + j, 4)
            prepare(g)
            leave(g, 0, 32)
        leave(mine, 0, place)
        dst[me] = src[me]

    def gather(take, src, dst, send, recv):
        def blocks(count, g):
            return pltpu.make_async_remote_copy(
                src.at[pl.ds(0, count)],
                dst.at[pl.ds(0, count)],
                send,
                wide_sem.at[recv + g],
                device_id=coords(lax.rem(me + 1, DEV)),
                device_id_type=MESH,
            )

        for j in range(4):
            g = lax.rem(mine + 3 - j, 4)
            blocks(31 if j == 3 else 32, g).wait_recv()
            take(g)
        blocks(DEV - 1, 0).wait_send()

    def put_state(row, lane, piece):
        state[row : row + 8, lane : lane + 128] = piece

    pixels_to_patches(lambda r, c: image[r : r + 8, c : c + 128], put_state)
    lane = lax.broadcasted_iota(jnp.int32, (128, 128), 1)
    low = (lane // 32) % 2 == 0
    sign = jnp.where(lane < 64, -1.0, 1.0)
    right = lax.rem(tx + 1, NTX)
    left = lax.rem(tx + NTX - 1, NTX)
    below = lax.rem(ty + 1, NTY)
    above = lax.rem(ty + NTY - 1, NTY)

    key = lax.broadcasted_iota(jnp.int32, (1, 64), 1)
    query = lax.broadcasted_iota(jnp.int32, (128, 1), 0) % 64
    returning = []

    def roll_back(t):
        for copy in returning[t]:
            copy.wait()
        for p in range(8):
            for wi in range(2):
                around[8 + wi * 8 + p, 0:8, :] = to_right[t, wi, p * 8 : p * 8 + 8, :].astype(F32)
            for wk in range(4):
                around[p, 8 + wk * 8 : 16 + wk * 8, :] = to_below[t, wk, p * 8 : p * 8 + 8, :].astype(F32)
            around[p, 0:8, :] = to_corner[t, p * 8 : p * 8 + 8, :].astype(F32)
        for i in range(ROWS):
            rows = slice(i * COLS, i * COLS + COLS)
            piece = pltpu.roll(around[8 + i - offsets[t, 0]], COLS + offsets[t, 1], 0)[:COLS]
            state[rows, :] = half[rows, :] - SIGMAS[t] * piece

    for t in range(STEPS):
        base = t * 16

        if t == 0:
            sa[...] = state[...].astype(BF16).reshape(NTX, 64, PIX)
            pl.semaphore_wait(barrier, NTX + NTY - 2)
            for o in range(1, NTY):
                pl.semaphore_signal(arrived, inc=1, device_id=(lax.rem(ty + o, NTY), tx), device_id_type=MESH)
        arrive = begin(ty, tx, sa, ra.at[t], send_sem.at[base], recv_sem.at[base])
        cos2, sin2 = tw2.at[0], tw2.at[1]
        if t == 0:
            need("key_mask")
            spot = lax.broadcasted_iota(jnp.int32, (64, 1), 0)
            mask_lane = lax.broadcasted_iota(jnp.int32, (64, COLS), 1)
            for w in range(8):
                wk, wi = w // 2, w % 2
                lines = [jnp.broadcast_to(key_mask[wi * 8 + p : wi * 8 + p + 1, :], (8, COLS)) for p in range(8)]
                lines = jnp.concatenate(lines, axis=0)
                kept = jnp.sum(jnp.where(mask_lane == wk * 8 + spot % 8, lines, 0).astype(F32), axis=1, keepdims=True)
                kept = jnp.sum(jnp.where(spot == key, kept, 0.0), axis=0, keepdims=True)
                bias0[w] = jnp.where((kept == 1.0) | (key == query), 0.0, -1e30)
        else:
            moved = offsets[t - 1, 0]
            eight = lax.broadcasted_iota(jnp.int32, (128, 8), 1)
            pc = jnp.sum(jnp.where(eight == moved, ph[0], 0.0), axis=1, keepdims=True)
            ps = jnp.sum(jnp.where(eight == moved, ph[1], 0.0), axis=1, keepdims=True)
            cos2 = tw2[0] * pc + tw2[1] * sign * ps
            sin2 = tw2[1] * pc - tw2[0] * sign * ps
            odd = lax.broadcasted_iota(jnp.int32, (128, 1), 0) % 2 * (moved % 2)
            flip = 1.0 - 2.0 * odd.astype(F32)
        arrive()
        got = ra[t]
        slab = jnp.concatenate([got[:, :32, :].reshape(256, PIX), got[:, 32:, :].reshape(256, PIX)], axis=1)
        if t > 0:
            slab = pltpu.roll(slab.astype(F32), offsets[t - 1, 1], 0).astype(BF16)
        need("w1", "tw1")
        cos1 = jnp.concatenate([tw1[0], tw1[0]], axis=1)
        sin1 = jnp.concatenate([tw1[1], tw1[1]], axis=1)
        part = mm(w1[...], slab)
        pr, pi = part[:256], part[256:]
        part = jnp.concatenate([pr * cos1 + pi * sin1, pi * cos1 - pr * sin1], axis=1).astype(BF16)
        need("f1")
        if t == 0:
            pl.semaphore_wait(arrived, NTY - 1)

        def leave_rows(g):
            out = mm(part, f1[:, pl.ds(pl.multiple_of(g * 256, 256), 256)])
            for e in range(2):
                a0 = out[0:128, e * 128 : e * 128 + 128]
                a1 = out[128:256, e * 128 : e * 128 + 128]
                at = g * 32 + e * 16
                sb[pl.ds(at, 8)] = jnp.where(low, a0, pltpu.roll(a1, 32, 1)).astype(BF16).reshape(8, 16, 128)
                sb[pl.ds(at + 8, 8)] = jnp.where(low, pltpu.roll(a0, 96, 1), a1).astype(BF16).reshape(8, 16, 128)

        scatter(leave_rows, sb, rb.at[t], send_sem.at[base + 1], t * 8)

        if t == 0:
            need("gains", "observed", "weight", "w2", "w3", "tw2", "tw3", "m2", "m3", "ph")
            for q in range(4):
                rows = slice(q * 8, q * 8 + 8)
                for v in range(32):
                    cols = slice(v * 128, v * 128 + 128)
                    gr, gi = gains[0, rows, cols], gains[1, rows, cols]
                    zr, zi = observed[0, rows, cols], observed[1, rows, cols]
                    wt = weight[rows, cols]
                    at = slice((q * 32 + v) * 8, (q * 32 + v) * 8 + 8)
                    xf[at, :] = (wt * (gr * gr + gi * gi)) * (1.0 / N)
                    xf[1024 + at.start : 1024 + at.stop, :] = wt * (gr * zr + gi * zi)
                    xg[at, :] = wt * (gr * zi - gi * zr)
            for q in range(4):
                h, mh = q // 2, q % 2
                for ml in range(8):
                    cols = slice((mh * 8 + ml) * 128, (mh * 8 + ml) * 128 + 128)
                    abr[0, h * 32 : h * 32 + 32, cols] = xf[pl.ds(q * 256 + ml, 32, stride=8), :]
                    abr[1, h * 32 : h * 32 + 32, cols] = xf[pl.ds(1024 + q * 256 + ml, 32, stride=8), :]
                    abr[2, h * 32 : h * 32 + 32, cols] = xg[pl.ds(q * 256 + ml, 32, stride=8), :]

        def take_rows(g):
            at = pl.multiple_of(g * 512, 512)
            xf[pl.ds(at, 512), :] = rb[t, pl.ds(g * 32, 32)].reshape(512, 128).astype(F32)

        gather(take_rows, sb, rb.at[t], send_sem.at[base + 1], t * 8)
        for m4 in range(0, 16, 4):
            xs = [xf[pl.ds(m4 + n, DEV, stride=16), :] for n in range(4)]
            turned = [pltpu.roll(x, 64, 1) * sign for x in xs]
            both = jnp.concatenate([jnp.concatenate(xs, axis=1), jnp.concatenate(turned, axis=1)], axis=0).astype(BF16)
            y = mm(w2[...], both)
            ys = [y[:, n * 128 : n * 128 + 128] for n in range(4)]
            ys = [x * cos2[...] + pltpu.roll(x, 64, 1) * sin2[...] for x in ys]
            z = nt(m2[...], jnp.concatenate(ys, axis=0).astype(BF16))
            if t > 0:
                z = z * flip
            cols = slice(m4 * 128, m4 * 128 + 512)
            fac = abr[0, :, cols]
            back = jnp.concatenate([fac * z[:64] - abr[1, :, cols], fac * z[64:] - abr[2, :, cols]], axis=0)
            v = mm(m3[...], back.astype(BF16))
            rows = []
            for n in range(4):
                vr, vi = v[:64, n * 128 : n * 128 + 128], v[64:, n * 128 : n * 128 + 128]
                xr = vr * tw3[0] - vi * tw3[1]
                xi = vi * tw3[0] + vr * tw3[1]
                rows.append(jnp.concatenate([jnp.concatenate([xr, xi], axis=0), jnp.concatenate([-xi, xr], axis=0)], axis=1))
            vst[m4 * 128 : m4 * 128 + 512, :] = jnp.concatenate(rows, axis=0).astype(BF16)

        def leave_cols(g):
            u = nt(w3[pl.ds(pl.multiple_of(g * 32, 32), 32), :], vst[...])
            for m in range(16):
                xg[pl.ds(m, 32, stride=16), :] = u[:, m * 128 : m * 128 + 128]
            sc[pl.ds(g * 32, 32)] = xg[0:512, :].astype(BF16).reshape(32, 16, 128)

        scatter(leave_cols, sc, rc.at[t], send_sem.at[base + 2], t * 8 + 4)
        need("f2", "w4")
        sums = []

        def take_cols(g):
            low_half, high_half = [], []
            for e in range(2):
                at = g * 32 + e * 16
                r0 = rc[t, pl.ds(at, 8)].reshape(128, 128).astype(F32)
                r1 = rc[t, pl.ds(at + 8, 8)].reshape(128, 128).astype(F32)
                low_half.append(jnp.where(low, r0, pltpu.roll(r1, 32, 1)))
                high_half.append(jnp.where(low, pltpu.roll(r0, 96, 1), r1))
            both = jnp.concatenate([jnp.concatenate(low_half, axis=1), jnp.concatenate(high_half, axis=1)], axis=0)
            term = mm(both.astype(BF16), f2[pl.ds(pl.multiple_of(g * 256, 256), 256), :])
            sums.append(sums[-1] + term if sums else term)

        gather(take_cols, sc, rc.at[t], send_sem.at[base + 2], t * 8 + 4)
        part = sums[-1]
        pr, pi = part[:, :512], part[:, 512:]
        part = jnp.concatenate([pr * cos1 - pi * sin1, pi * cos1 + pr * sin1], axis=0)
        part = part.astype(BF16)

        gradient = []
        for hf in range(2):
            for n in range(NTX):
                y = mm(w4[n * 32 + hf * 16 : n * 32 + hf * 16 + 16, :], part).astype(BF16)
                sd[hf, n, 0:16, :] = y[:, :PIX]
                sd[hf, n, 16:32, :] = y[:, PIX:]
            gradient.append(
                begin(ty, tx, sd.at[hf], rd.at[t, hf], send_sem.at[base + 3 + hf], recv_sem.at[base + 3 + hf])
            )

        need("w_embed", "w_qkv", "w_proj", "w_up", "w_down", "w_unembed", "norm_gains")
        sr = offsets[t, 0]
        sc_ = offsets[t, 1]
        sends = []

        def send(src, dst, who, n):
            copy = pltpu.make_async_remote_copy(
                src, dst, send_sem.at[base + n], recv_sem.at[base + n], device_id=who, device_id_type=MESH
            )
            copy.start()
            sends.append(copy)

        if t > 0:
            roll_back(t - 1)
        for hf in range(2):
            gradient[hf]()
            grad = rd[t, hf].astype(F32)
            pieces = []
            for w in range(hf * 4, hf * 4 + 4):
                wk, wi = w // 2, w % 2
                for p in range(8):
                    i = wi * 8 + p
                    at = i * COLS + wk * 8
                    move = grad[i // 2, (i % 2) * 16 + (wk % 2) * 8 : (i % 2) * 16 + (wk % 2) * 8 + 8, :]
                    piece = state[at : at + 8, :] - STEP_SIZES[t] * move
                    half[at : at + 8, :] = piece
                    pieces.append(piece)
            patches = jnp.concatenate(pieces, axis=0).astype(BF16)
            rows = slice(hf * 256, hf * 256 + 256)
            flow[rows, :] = mm(patches, w_embed[...]).astype(BF16).astype(F32)
            swin_rows(flow, qkv, att, hf * 4, 4, lambda n: bias0[n], w_qkv, w_proj, w_up, w_down, norm_gains, 0)
            first[rows, :] = flow[rows, :].astype(BF16)
            if hf == 0:
                send(first.at[pl.ds(0, 128)], from_right.at[t], (ty, left), 5)
                send(first.at[pl.ds(0, 64)], from_corner.at[t], (above, left), 6)
            for wk in (2 * hf, 2 * hf + 1):
                send(first.at[pl.ds(wk * 128, 64)], from_below.at[t, wk], (above, tx), 7 + wk)
            for w in range(hf * 4, hf * 4 + 4):
                wk, wi = w // 2, w % 2
                for p in range(8):
                    row = w * 64 + p * 8
                    padded[wi * 8 + p, wk * 8 : wk * 8 + 8, :] = first[row : row + 8, :].astype(F32)

        if t + 1 < STEPS:

            def add_noise(row, lane, piece):
                half[row : row + 8, lane : lane + 128] = half[row : row + 8, lane : lane + 128] + SIGMAS[t + 1] * piece

            need("noise")
            pixels_to_patches(lambda r, c: noise[r : r + 8, c : c + 128], add_noise)
            hb[...] = half[...].astype(BF16)
            hr[...] = jnp.concatenate([half[i * COLS : i * COLS + 8, :] for i in range(ROWS)], axis=0).astype(BF16)
            early = [
                pltpu.make_async_remote_copy(
                    src, dst, send_sem.at[32 + n], recv_sem.at[32 + n], device_id=who, device_id_type=MESH
                )
                for n, (src, dst, who) in enumerate(
                    [
                        (hb.at[pl.ds(0, 256)], hn_below, (above, tx)),
                        (hr, hn_right, (ty, left)),
                        (hr.at[pl.ds(0, 64)], hn_corner, (above, left)),
                    ]
                )
            ]
            for copy in early:
                copy.start()
            for i in range(ROWS):
                hpad[i, 0:COLS, :] = half[i * COLS : i * COLS + COLS, :]

        def bias1(n):
            wi, wk = n // 4, n % 4

            def label(x):
                return 3 * region(ty * ROWS + wi * 8 + x // 8, sr) + region(tx * COLS + wk * 8 + x % 8, sc_)

            return jnp.where(label(key) == label(query), 0.0, -1e30)

        def shifted(start, count):
            swin_rows(flow, qkv, att, start, count, bias1, w_qkv, w_proj, w_up, w_down, norm_gains, 1)
            rows = slice(start * 64, (start + count) * 64)
            est = mm(flow[rows, :].astype(BF16), w_unembed[...])
            eb[start : start + count] = est.astype(BF16).reshape(count, 64, PIX)
            return est

        def place(est, start, count):
            for n in range(start, start + count):
                wi, wk = n // 4, n % 4
                for p in range(8):
                    row = (n - start) * 64 + p * 8
                    around[8 + wi * 8 + p, 8 + wk * 8 : 16 + wk * 8, :] = est[row : row + 8, :]

        for p in range(8):
            rolled = pltpu.roll(padded[p + sr, 0:COLS, :], COLS - sc_, 0)
            for wk in range(3):
                row = wk * 64 + p * 8
                flow[row : row + 8, :] = rolled[wk * 8 : wk * 8 + 8, :]
        place(shifted(0, 3), 0, 3)
        for copy in sends:
            copy.wait()
        sends.clear()
        for p in range(8):
            for wk in range(4):
                padded[16 + p, wk * 8 : wk * 8 + 8, :] = from_below[t, wk, p * 8 : p * 8 + 8, :].astype(F32)
            for wi in range(2):
                at = wi * 64 + p * 8
                padded[wi * 8 + p, 32:40, :] = from_right[t, at : at + 8, :].astype(F32)
            padded[16 + p, 32:40, :] = from_corner[t, p * 8 : p * 8 + 8, :].astype(F32)
        for i in range(ROWS):
            rolled = pltpu.roll(padded[i + sr], COLS + 8 - sc_, 0)
            for wk in range(3 if i < 8 else 0, 4):
                row = ((i // 8 * 4 + wk) * 8 + i % 8) * 8
                flow[row : row + 8, :] = rolled[wk * 8 : wk * 8 + 8, :]
        est = shifted(3, 5)
        back = []
        for n, (src, dst, who) in enumerate(
            [
                (eb.at[pl.ds(4, 4)], to_below.at[t], (below, tx)),
                (eb.at[3], to_right.at[t, 0], (ty, right)),
                (eb.at[7], to_right.at[t, 1], (ty, right)),
                (eb.at[7], to_corner.at[t], (below, right)),
            ]
        ):
            copy = pltpu.make_async_remote_copy(
                src, dst, send_sem.at[base + 11 + n], recv_sem.at[base + 11 + n], device_id=who, device_id_type=MESH
            )
            copy.start()
            back.append(copy)
        returning.append(back)
        place(est, 3, 5)
        if t + 1 < STEPS:
            for copy in early:
                copy.wait()
            for p in range(8):
                hpad[16 + p, 0:COLS, :] = hn_below[p * COLS : p * COLS + COLS, :].astype(F32)
                hpad[16 + p, COLS : COLS + 8, :] = hn_corner[p * 8 : p * 8 + 8, :].astype(F32)
            for i in range(ROWS):
                hpad[i, COLS : COLS + 8, :] = hn_right[i * 8 : i * 8 + 8, :].astype(F32)
            for i in range(ROWS):
                ahead = pltpu.roll(hpad[i + sr], COLS + 8 - sc_, 0)[:COLS]
                ahead = ahead - SIGMAS[t] * around[8 + i, 8 : 8 + COLS, :]
                sa[i // 2, i % 2 * COLS : i % 2 * COLS + COLS, :] = ahead.astype(BF16)
        else:
            roll_back(t)

            def give(row, lane, piece):
                out[row : row + 8, lane : lane + 128] = piece

            patches_to_pixels(lambda r, c: state[r : r + 8, c : c + 128], give)


def per_device(consts, image, noise, offsets, key_mask, gains, observed, vis_weight, w_embed, w_qkv, w_proj, w_up, w_down, w_unembed, norm_gains):
    w1, w4, tw1, f1, f2, w2, w3, tw2, tw3, m2, m3, ph = consts
    arrays = dict(
        image=image, key_mask=key_mask, w1=w1, tw1=tw1, f1=f1, gains=gains, observed=observed, weight=vis_weight,
        w2=w2, w3=w3, tw2=tw2, tw3=tw3, m2=m2, m3=m3, f2=f2, w4=w4, ph=ph, norm_gains=norm_gains, w_embed=w_embed,
        w_qkv=w_qkv, w_proj=w_proj, w_up=w_up, w_down=w_down, w_unembed=w_unembed, noise=noise,
    )
    moved = [arrays[name] for name in NAMES]
    V = pltpu.VMEM
    held = [V(x.shape[1:] if name == "noise" else x.shape, x.dtype) for name, x in zip(NAMES, moved)]
    scratch = held + [
        V((TOKENS, PIX), F32),
        V((TOKENS, PIX), F32),
        V((NTX, 64, PIX), BF16),
        V((STEPS, NTX, 64, PIX), BF16),
        V((DEV, 16, 128), BF16),
        V((STEPS, DEV, 16, 128), BF16),
        V((DEV, 16, 128), BF16),
        V((STEPS, DEV, 16, 128), BF16),
        V((2, NTX, 32, PIX), BF16),
        V((STEPS, 2, NTX, 32, PIX), BF16),
        V((DEV * 16, 128), F32),
        V((1024, 128), F32),
        V((3, 64, 2048), F32),
        V((TOKENS, D), F32),
        V((TOKENS, 3 * D), BF16),
        V((TOKENS, D), BF16),
        V((TOKENS, D), BF16),
        V((ROWS + 8, COLS + 8, D), F32),
        V((ROWS + 8, COLS + 8, PIX), F32),
        V((STEPS, 128, D), BF16),
        V((STEPS, 4, 64, D), BF16),
        V((STEPS, 64, D), BF16),
        V((STEPS, 2, 64, PIX), BF16),
        V((STEPS, 4, 64, PIX), BF16),
        V((STEPS, 64, PIX), BF16),
        V((8, 128, 64), F32),
        V((2048, 256), BF16),
        V((8, 64, PIX), BF16),
        V((TOKENS, PIX), BF16),
        V((128, PIX), BF16),
        V((ROWS + 8, COLS + 8, PIX), F32),
        V((256, PIX), BF16),
        V((128, PIX), BF16),
        V((64, PIX), BF16),
        pltpu.SemaphoreType.DMA((len(NAMES),)),
        pltpu.SemaphoreType.DMA((STEPS * 16 + 3,)),
        pltpu.SemaphoreType.DMA((STEPS * 16 + 3,)),
        pltpu.SemaphoreType.DMA((STEPS * 2 * 4,)),
        pltpu.SemaphoreType.REGULAR,
    ]
    stepped = pl.pallas_call(
        kernel,
        out_shape=jax.ShapeDtypeStruct(image.shape, F32),
        in_specs=[pl.BlockSpec(memory_space=pltpu.SMEM)] + [pl.BlockSpec(memory_space=pl.ANY)] * len(NAMES),
        out_specs=pl.BlockSpec(memory_space=pltpu.VMEM),
        scratch_shapes=scratch,
        compiler_params=pltpu.CompilerParams(collective_id=0, has_side_effects=True, vmem_limit_bytes=60 * 2**20),
    )(offsets, *moved)
    return stepped + SIGMAS[STEPS] * noise[STEPS - 1]


def solution(mesh):
    consts = tables()
    in_specs = (
        P("ty", "tx"),
        P(None, "ty", "tx"),
        P(),
        P("ty", "tx"),
        P(None, ("ty", "tx"), None),
        P(None, ("ty", "tx"), None),
        P(("ty", "tx"), None),
        P(),
        P(),
        P(),
        P(),
        P(),
        P(),
        P(),
    )
    consts_specs = (P(),) * len(consts)
    mapped = jax.shard_map(
        lambda c, *args: per_device(c, *args),
        mesh=mesh,
        in_specs=(consts_specs,) + in_specs,
        out_specs=P("ty", "tx"),
        check_vma=False,
    )
    return lambda *args: mapped(tuple(jnp.asarray(c) for c in consts), *args)
```

```python
import functools
import math

import jax
import jax.numpy as jnp
import numpy as np
from jax import lax
from jax.experimental import pallas as pl
from jax.experimental.pallas import tpu as pltpu
from jax.sharding import PartitionSpec as P

N = 4096
WIN = 8
D = 512
HEADS = 8
FF = 2048
STEPS = 2
NTY = 16
NTX = 8
DEV = NTY * NTX
ROWS = 16
COLS = 32
TOKENS = ROWS * COLS
PIX = 256
SIDE = 256
SIGMAS = (0.8, 0.5, 0.3)
STEP_SIZES = (0.9, 0.7)
EPSILON = 1e-05
MESH = pl.DeviceIdType.MESH
F32 = jnp.float32
BF16 = jnp.bfloat16


def tables():
    k1 = np.array([32 * t + 16 * h + m for h in range(2) for t in range(8) for m in range(16)])
    k = np.arange(256)
    ang = 2 * np.pi * ((k1[:, None] * k[None, :]) % 256) / 256
    w1 = np.concatenate([np.cos(ang), -np.sin(ang)], axis=0)
    w4 = w1.T.reshape(8, 2, 16, 512).transpose(1, 0, 2, 3).reshape(256, 512)
    b = np.tile(np.arange(16), 16)
    ang = 2 * np.pi * (k1[:, None] * b[None, :]) / 4096
    tw1 = np.stack([np.cos(ang), np.sin(ang)])
    eye = np.eye(32)
    b16 = np.arange(16)
    ang = 2 * np.pi * ((b16[:, None] * b16[None, :]) % 16) / 16
    wr, wi = np.cos(ang), -np.sin(ang)
    core = np.zeros((2, 16, 16, 2))
    core[0, :, :, 0], core[0, :, :, 1] = wr, wi
    core[1, :, :, 0], core[1, :, :, 1] = -wi, wr
    core = core.reshape(2, 16, 8, 2, 2)
    f1 = np.einsum("cbpld,xy->cxbpdly", core, eye).reshape(1024, 1024)
    wi = -wi
    core = np.zeros((16, 2, 2, 16))
    core[:, 0, 0], core[:, 0, 1] = wr, wi
    core[:, 1, 0], core[:, 1, 1] = -wi, wr
    core = core.reshape(8, 2, 2, 2, 16)
    f2 = np.einsum("plcdb,xy->pclxdyb", core, eye).reshape(1024, 1024)
    u = np.arange(128)
    ang = 2 * np.pi * ((u[:, None] * u[None, :]) % 128) / 128
    w2 = np.concatenate([np.cos(ang), -np.sin(ang)], axis=1)
    w3 = np.concatenate([np.cos(ang), np.sin(ang)], axis=1)
    rho = np.arange(32)
    ang = 2 * np.pi * (rho[:, None] * u[None, :]) / 4096
    c, s = np.cos(ang), np.sin(ang)
    tw2c = np.concatenate([c, c, c, c], axis=0).T
    tw2s = np.concatenate([s, s, -s, -s], axis=0).T
    tw2 = np.stack([tw2c, tw2s])
    tw3 = np.stack([np.concatenate([c, c]), np.concatenate([s, s])]) / N
    ang = 2 * np.pi * ((rho[:, None] * rho[None, :]) % 32) / 32
    wr, wi = np.cos(ang), -np.sin(ang)
    eye2 = np.eye(2)

    def block(wr, wi):
        return np.block([[np.kron(eye2, wr), np.kron(eye2, -wi)], [np.kron(eye2, wi), np.kron(eye2, wr)]])

    m2 = block(wr, wi)
    m3 = block(wr, -wi)
    ang = 2 * np.pi * (u[:, None] * np.arange(8)[None, :]) / 256
    ph = np.stack([np.cos(ang), np.sin(ang)])
    half = lambda x: np.asarray(x, np.float32).astype(BF16)
    full = lambda x: np.asarray(x, np.float32)
    return (half(w1), half(w4), full(tw1), half(f1), half(f2), half(w2), half(w3), full(tw2), full(tw3), half(m2), half(m3), full(ph))


def mm(a, b):
    return jnp.dot(a, b, preferred_element_type=F32)


def nt(a, b):
    return lax.dot_general(a, b, (((1,), (1,)), ((), ())), preferred_element_type=F32)


def swap_blocks(x):
    sub = lax.broadcasted_iota(jnp.int32, x.shape, 1)
    lane = lax.broadcasted_iota(jnp.int32, x.shape, 2) // 16
    for d in (4, 2, 1):
        bs = (sub // d) % 2
        bl = (lane // d) % 2
        after = pltpu.roll(pltpu.roll(x, 8 - d, 1), 16 * d, 2)
        if d == 4:
            x = jnp.where(bs == bl, x, after)
        else:
            before = pltpu.roll(pltpu.roll(x, d, 1), 128 - 16 * d, 2)
            x = jnp.where(bs == bl, x, jnp.where(bs == 0, after, before))
    return x


def pixels_to_patches(read, write):
    for i in range(ROWS):
        pieces = [read(i * 16 + ah * 8, kh * 128) for kh in range(4) for ah in range(2)]
        out = swap_blocks(jnp.stack(pieces))
        for kh in range(4):
            for ah in range(2):
                write(i * COLS + kh * 8, ah * 128, out[kh * 2 + ah])


def patches_to_pixels(read, write):
    for i in range(ROWS):
        pieces = [read(i * COLS + kh * 8, ah * 128) for kh in range(4) for ah in range(2)]
        out = swap_blocks(jnp.stack(pieces))
        for kh in range(4):
            for ah in range(2):
                write(i * 16 + ah * 8, kh * 128, out[kh * 2 + ah])


def coords(d):
    return (d // NTX, lax.rem(d, NTX))


def begin(ty, tx, src, dst, send_sem, recv_sem):
    for o in (1, 7, 2, 6, 3, 5, 4):
        n = lax.rem(tx + o, NTX)
        pltpu.make_async_remote_copy(
            src.at[n], dst.at[tx], send_sem, recv_sem, device_id=(ty, n), device_id_type=MESH
        ).start()
    dst[tx] = src[tx]

    def finish():
        rest = pltpu.make_async_remote_copy(
            src.at[pl.ds(0, NTX - 1)],
            dst.at[pl.ds(0, NTX - 1)],
            send_sem,
            recv_sem,
            device_id=(ty, lax.rem(tx + 1, NTX)),
            device_id_type=MESH,
        )
        rest.wait_send()
        rest.wait_recv()

    return finish


def layer_norm(values, gain):
    centre = jnp.mean(values, axis=-1, keepdims=True)
    shifted = values - centre
    spread = jnp.mean(shifted * shifted, axis=-1, keepdims=True)
    return shifted * lax.rsqrt(spread + EPSILON) * gain


def gelu(v):
    return 0.5 * v * (1.0 + jnp.tanh(math.sqrt(2.0 / math.pi) * (v + 0.044715 * (v * v * v))))


def swin_rows(flow, qkv, att, start, count, bias_of, w_qkv, w_proj, w_up, w_down, gains, j):
    rows = slice(start * 64, (start + count) * 64)
    normed = layer_norm(flow[rows, :], gains[j, 0:1, :]).astype(BF16)
    qkv[rows, :] = mm(normed, w_qkv[j]).astype(BF16)
    lane = lax.broadcasted_iota(jnp.int32, (1, 128), 1)
    low = lane < 64
    pick_low = jnp.where(low, 0.125, 0.0).astype(BF16)
    pick_high = jnp.where(low, 0.0, 0.125).astype(BF16)
    for n in range(start, start + count):
        at = slice(n * 64, n * 64 + 64)
        bias = bias_of(n)
        for pair in range(4):
            cols = slice(pair * 128, pair * 128 + 128)
            q = qkv[at, cols]
            k = qkv[at, D + pair * 128 : D + pair * 128 + 128]
            v = qkv[at, 2 * D + pair * 128 : 2 * D + pair * 128 + 128]
            both = jnp.concatenate([q * pick_low, q * pick_high], axis=0)
            scores = nt(both, k) + bias
            weights = jnp.exp(scores - jnp.max(scores, axis=1, keepdims=True))
            probs = weights * (1.0 / jnp.sum(weights, axis=1, keepdims=True))
            mixed = mm(probs.astype(BF16), v)
            att[at, cols] = jnp.where(low, mixed[:64], mixed[64:]).astype(BF16)
    after = flow[rows, :] + mm(att[rows, :], w_proj[j])
    normed = layer_norm(after, gains[j, 1:2, :]).astype(BF16)
    for c in range(0, FF, 512):
        hidden = gelu(mm(normed, w_up[j, :, c : c + 512])).astype(BF16)
        after = after + mm(hidden, w_down[j, c : c + 512, :])
    flow[rows, :] = after


def region(index, shift):
    return jnp.where(index < SIDE - WIN, 0, jnp.where(index < SIDE - shift, 1, 2))


NAMES = (
    "image", "key_mask", "w1", "tw1", "f1", "gains", "observed", "weight", "w2", "w3", "tw2", "tw3", "m2", "m3", "f2", "w4", "ph",
    "norm_gains", "w_embed", "w_qkv", "w_proj", "w_up", "w_down", "w_unembed", "noise",
)


def kernel(offsets, *refs):
    count = len(NAMES)
    sources = refs[:count]
    out = refs[count]
    held = refs[count + 1 : 2 * count + 1]
    (
        image, key_mask, w1, tw1, f1, gains, observed, weight, w2, w3, tw2, tw3, m2, m3, f2, w4, ph,
        norm_gains, w_embed, w_qkv, w_proj, w_up, w_down, w_unembed, noise,
    ) = held
    (
        state, half, sa, ra, sb, rb, sc, rc, sd, rd, xf, xg, abr, flow, qkv, att, first, padded, around,
        from_right, from_below, from_corner, to_right, to_below, to_corner, bias0, vst, eb, hb, hr, hpad, hn_below, hn_right, hn_corner, load_sem, send_sem, recv_sem, wide_sem, arrived,
    ) = refs[2 * count + 1 :]
    ty = lax.axis_index("ty")
    tx = lax.axis_index("tx")
    me = ty * NTX + tx
    barrier = pltpu.get_barrier_semaphore()

    for o in range(1, NTX):
        pl.semaphore_signal(barrier, inc=1, device_id=(ty, lax.rem(tx + o, NTX)), device_id_type=MESH)
    for o in range(1, NTY):
        pl.semaphore_signal(barrier, inc=1, device_id=(lax.rem(ty + o, NTY), tx), device_id_type=MESH)
    loads = {}
    for n, name in enumerate(NAMES):
        source = sources[n].at[0] if name == "noise" else sources[n]
        loads[name] = pltpu.make_async_copy(source, held[n], load_sem.at[n])
        loads[name].start()

    def need(*names):
        for name in names:
            if name in loads:
                loads.pop(name).wait()

    need("image")
    mine = me // 32

    def scatter(prepare, src, dst, send, recv):
        place = lax.rem(me, 32)

        def leave(g, first, last):
            def one(o, carry):
                d = g * 32 + o
                pltpu.make_async_remote_copy(
                    src.at[d], dst.at[me], send, wide_sem.at[recv + mine], device_id=coords(d), device_id_type=MESH
                ).start()
                return carry

            lax.fori_loop(first, last, one, 0)

        prepare(mine)
        leave(mine, place + 1, 32)
        for j in range(1, 4):
            g = lax.rem(mine + j, 4)
            prepare(g)
            leave(g, 0, 32)
        leave(mine, 0, place)
        dst[me] = src[me]

    def gather(take, src, dst, send, recv):
        def blocks(count, g):
            return pltpu.make_async_remote_copy(
                src.at[pl.ds(0, count)],
                dst.at[pl.ds(0, count)],
                send,
                wide_sem.at[recv + g],
                device_id=coords(lax.rem(me + 1, DEV)),
                device_id_type=MESH,
            )

        for j in range(4):
            g = lax.rem(mine + 3 - j, 4)
            blocks(31 if j == 3 else 32, g).wait_recv()
            take(g)
        blocks(DEV - 1, 0).wait_send()

    def put_state(row, lane, piece):
        state[row : row + 8, lane : lane + 128] = piece

    pixels_to_patches(lambda r, c: image[r : r + 8, c : c + 128], put_state)
    lane = lax.broadcasted_iota(jnp.int32, (128, 128), 1)
    low = (lane // 32) % 2 == 0
    sign = jnp.where(lane < 64, -1.0, 1.0)
    right = lax.rem(tx + 1, NTX)
    left = lax.rem(tx + NTX - 1, NTX)
    below = lax.rem(ty + 1, NTY)
    above = lax.rem(ty + NTY - 1, NTY)

    key = lax.broadcasted_iota(jnp.int32, (1, 64), 1)
    query = lax.broadcasted_iota(jnp.int32, (128, 1), 0) % 64
    returning = []

    def roll_back(t):
        for copy in returning[t]:
            copy.wait()
        for p in range(8):
            for wi in range(2):
                around[8 + wi * 8 + p, 0:8, :] = to_right[t, wi, p * 8 : p * 8 + 8, :].astype(F32)
            for wk in range(4):
                around[p, 8 + wk * 8 : 16 + wk * 8, :] = to_below[t, wk, p * 8 : p * 8 + 8, :].astype(F32)
            around[p, 0:8, :] = to_corner[t, p * 8 : p * 8 + 8, :].astype(F32)
        for i in range(ROWS):
            rows = slice(i * COLS, i * COLS + COLS)
            piece = pltpu.roll(around[8 + i - offsets[t, 0]], COLS + offsets[t, 1], 0)[:COLS]
            state[rows, :] = half[rows, :] - SIGMAS[t] * piece

    for t in range(STEPS):
        base = t * 16

        if t == 0:
            sa[...] = state[...].astype(BF16).reshape(NTX, 64, PIX)
            pl.semaphore_wait(barrier, NTX + NTY - 2)
            for o in range(1, NTY):
                pl.semaphore_signal(arrived, inc=1, device_id=(lax.rem(ty + o, NTY), tx), device_id_type=MESH)
        arrive = begin(ty, tx, sa, ra.at[t], send_sem.at[base], recv_sem.at[base])
        cos2, sin2 = tw2.at[0], tw2.at[1]
        if t == 0:
            need("key_mask")
            spot = lax.broadcasted_iota(jnp.int32, (64, 1), 0)
            mask_lane = lax.broadcasted_iota(jnp.int32, (64, COLS), 1)
            for w in range(8):
                wk, wi = w // 2, w % 2
                lines = [jnp.broadcast_to(key_mask[wi * 8 + p : wi * 8 + p + 1, :], (8, COLS)) for p in range(8)]
                lines = jnp.concatenate(lines, axis=0)
                kept = jnp.sum(jnp.where(mask_lane == wk * 8 + spot % 8, lines, 0).astype(F32), axis=1, keepdims=True)
                kept = jnp.sum(jnp.where(spot == key, kept, 0.0), axis=0, keepdims=True)
                bias0[w] = jnp.where((kept == 1.0) | (key == query), 0.0, -1e30)
        else:
            moved = offsets[t - 1, 0]
            eight = lax.broadcasted_iota(jnp.int32, (128, 8), 1)
            pc = jnp.sum(jnp.where(eight == moved, ph[0], 0.0), axis=1, keepdims=True)
            ps = jnp.sum(jnp.where(eight == moved, ph[1], 0.0), axis=1, keepdims=True)
            cos2 = tw2[0] * pc + tw2[1] * sign * ps
            sin2 = tw2[1] * pc - tw2[0] * sign * ps
            odd = lax.broadcasted_iota(jnp.int32, (128, 1), 0) % 2 * (moved % 2)
            flip = 1.0 - 2.0 * odd.astype(F32)
        arrive()
        got = ra[t]
        slab = jnp.concatenate([got[:, :32, :].reshape(256, PIX), got[:, 32:, :].reshape(256, PIX)], axis=1)
        if t > 0:
            slab = pltpu.roll(slab.astype(F32), offsets[t - 1, 1], 0).astype(BF16)
        need("w1", "tw1")
        cos1 = jnp.concatenate([tw1[0], tw1[0]], axis=1)
        sin1 = jnp.concatenate([tw1[1], tw1[1]], axis=1)
        part = mm(w1[...], slab)
        pr, pi = part[:256], part[256:]
        part = jnp.concatenate([pr * cos1 + pi * sin1, pi * cos1 - pr * sin1], axis=1).astype(BF16)
        need("f1")
        if t == 0:
            pl.semaphore_wait(arrived, NTY - 1)

        def leave_rows(g):
            out = mm(part, f1[:, pl.ds(pl.multiple_of(g * 256, 256), 256)])
            for e in range(2):
                a0 = out[0:128, e * 128 : e * 128 + 128]
                a1 = out[128:256, e * 128 : e * 128 + 128]
                at = g * 32 + e * 16
                sb[pl.ds(at, 8)] = jnp.where(low, a0, pltpu.roll(a1, 32, 1)).astype(BF16).reshape(8, 16, 128)
                sb[pl.ds(at + 8, 8)] = jnp.where(low, pltpu.roll(a0, 96, 1), a1).astype(BF16).reshape(8, 16, 128)

        scatter(leave_rows, sb, rb.at[t], send_sem.at[base + 1], t * 8)

        if t == 0:
            need("gains", "observed", "weight", "w2", "w3", "tw2", "tw3", "m2", "m3", "ph")
            for q in range(4):
                rows = slice(q * 8, q * 8 + 8)
                for v in range(32):
                    cols = slice(v * 128, v * 128 + 128)
                    gr, gi = gains[0, rows, cols], gains[1, rows, cols]
                    zr, zi = observed[0, rows, cols], observed[1, rows, cols]
                    wt = weight[rows, cols]
                    at = slice((q * 32 + v) * 8, (q * 32 + v) * 8 + 8)
                    xf[at, :] = (wt * (gr * gr + gi * gi)) * (1.0 / N)
                    xf[1024 + at.start : 1024 + at.stop, :] = wt * (gr * zr + gi * zi)
                    xg[at, :] = wt * (gr * zi - gi * zr)
            for q in range(4):
                h, mh = q // 2, q % 2
                for ml in range(8):
                    cols = slice((mh * 8 + ml) * 128, (mh * 8 + ml) * 128 + 128)
                    abr[0, h * 32 : h * 32 + 32, cols] = xf[pl.ds(q * 256 + ml, 32, stride=8), :]
                    abr[1, h * 32 : h * 32 + 32, cols] = xf[pl.ds(1024 + q * 256 + ml, 32, stride=8), :]
                    abr[2, h * 32 : h * 32 + 32, cols] = xg[pl.ds(q * 256 + ml, 32, stride=8), :]

        def take_rows(g):
            at = pl.multiple_of(g * 512, 512)
            xf[pl.ds(at, 512), :] = rb[t, pl.ds(g * 32, 32)].reshape(512, 128).astype(F32)

        gather(take_rows, sb, rb.at[t], send_sem.at[base + 1], t * 8)
        for m4 in range(0, 16, 4):
            xs = [xf[pl.ds(m4 + n, DEV, stride=16), :] for n in range(4)]
            turned = [pltpu.roll(x, 64, 1) * sign for x in xs]
            both = jnp.concatenate([jnp.concatenate(xs, axis=1), jnp.concatenate(turned, axis=1)], axis=0).astype(BF16)
            y = mm(w2[...], both)
            ys = [y[:, n * 128 : n * 128 + 128] for n in range(4)]
            ys = [x * cos2[...] + pltpu.roll(x, 64, 1) * sin2[...] for x in ys]
            z = nt(m2[...], jnp.concatenate(ys, axis=0).astype(BF16))
            if t > 0:
                z = z * flip
            cols = slice(m4 * 128, m4 * 128 + 512)
            fac = abr[0, :, cols]
            back = jnp.concatenate([fac * z[:64] - abr[1, :, cols], fac * z[64:] - abr[2, :, cols]], axis=0)
            v = mm(m3[...], back.astype(BF16))
            rows = []
            for n in range(4):
                vr, vi = v[:64, n * 128 : n * 128 + 128], v[64:, n * 128 : n * 128 + 128]
                xr = vr * tw3[0] - vi * tw3[1]
                xi = vi * tw3[0] + vr * tw3[1]
                rows.append(jnp.concatenate([jnp.concatenate([xr, xi], axis=0), jnp.concatenate([-xi, xr], axis=0)], axis=1))
            vst[m4 * 128 : m4 * 128 + 512, :] = jnp.concatenate(rows, axis=0).astype(BF16)

        def leave_cols(g):
            u = nt(w3[pl.ds(pl.multiple_of(g * 32, 32), 32), :], vst[...])
            for m in range(16):
                xg[pl.ds(m, 32, stride=16), :] = u[:, m * 128 : m * 128 + 128]
            sc[pl.ds(g * 32, 32)] = xg[0:512, :].astype(BF16).reshape(32, 16, 128)

        scatter(leave_cols, sc, rc.at[t], send_sem.at[base + 2], t * 8 + 4)
        need("f2", "w4")
        sums = []

        def take_cols(g):
            low_half, high_half = [], []
            for e in range(2):
                at = g * 32 + e * 16
                r0 = rc[t, pl.ds(at, 8)].reshape(128, 128).astype(F32)
                r1 = rc[t, pl.ds(at + 8, 8)].reshape(128, 128).astype(F32)
                low_half.append(jnp.where(low, r0, pltpu.roll(r1, 32, 1)))
                high_half.append(jnp.where(low, pltpu.roll(r0, 96, 1), r1))
            both = jnp.concatenate([jnp.concatenate(low_half, axis=1), jnp.concatenate(high_half, axis=1)], axis=0)
            term = mm(both.astype(BF16), f2[pl.ds(pl.multiple_of(g * 256, 256), 256), :])
            sums.append(sums[-1] + term if sums else term)

        gather(take_cols, sc, rc.at[t], send_sem.at[base + 2], t * 8 + 4)
        part = sums[-1]
        pr, pi = part[:, :512], part[:, 512:]
        part = jnp.concatenate([pr * cos1 - pi * sin1, pi * cos1 + pr * sin1], axis=0)
        part = part.astype(BF16)

        gradient = []
        for hf in range(2):
            y = mm(w4[hf * 128 : hf * 128 + 128, :], part).astype(BF16)
            for n in range(NTX):
                sd[hf, n, 0:16, :] = y[n * 16 : n * 16 + 16, :PIX]
                sd[hf, n, 16:32, :] = y[n * 16 : n * 16 + 16, PIX:]
            gradient.append(
                begin(ty, tx, sd.at[hf], rd.at[t, hf], send_sem.at[base + 3 + hf], recv_sem.at[base + 3 + hf])
            )

        need("w_embed", "w_qkv", "w_proj", "w_up", "w_down", "w_unembed", "norm_gains")
        sr = offsets[t, 0]
        sc_ = offsets[t, 1]
        sends = []

        def send(src, dst, who, n):
            copy = pltpu.make_async_remote_copy(
                src, dst, send_sem.at[base + n], recv_sem.at[base + n], device_id=who, device_id_type=MESH
            )
            copy.start()
            sends.append(copy)

        if t > 0:
            roll_back(t - 1)
        for hf in range(2):
            gradient[hf]()
            grad = rd[t, hf].astype(F32)
            pieces = []
            for w in range(hf * 4, hf * 4 + 4):
                wk, wi = w // 2, w % 2
                for p in range(8):
                    i = wi * 8 + p
                    at = i * COLS + wk * 8
                    move = grad[i // 2, (i % 2) * 16 + (wk % 2) * 8 : (i % 2) * 16 + (wk % 2) * 8 + 8, :]
                    piece = state[at : at + 8, :] - STEP_SIZES[t] * move
                    half[at : at + 8, :] = piece
                    pieces.append(piece)
            patches = jnp.concatenate(pieces, axis=0).astype(BF16)
            rows = slice(hf * 256, hf * 256 + 256)
            flow[rows, :] = mm(patches, w_embed[...]).astype(BF16).astype(F32)
            swin_rows(flow, qkv, att, hf * 4, 4, lambda n: bias0[n], w_qkv, w_proj, w_up, w_down, norm_gains, 0)
            first[rows, :] = flow[rows, :].astype(BF16)
            if hf == 0:
                send(first.at[pl.ds(0, 128)], from_right.at[t], (ty, left), 5)
                send(first.at[pl.ds(0, 64)], from_corner.at[t], (above, left), 6)
            for wk in (2 * hf, 2 * hf + 1):
                send(first.at[pl.ds(wk * 128, 64)], from_below.at[t, wk], (above, tx), 7 + wk)
            for w in range(hf * 4, hf * 4 + 4):
                wk, wi = w // 2, w % 2
                for p in range(8):
                    row = w * 64 + p * 8
                    padded[wi * 8 + p, wk * 8 : wk * 8 + 8, :] = first[row : row + 8, :].astype(F32)

        if t + 1 < STEPS:

            def add_noise(row, lane, piece):
                half[row : row + 8, lane : lane + 128] = half[row : row + 8, lane : lane + 128] + SIGMAS[t + 1] * piece

            need("noise")
            pixels_to_patches(lambda r, c: noise[r : r + 8, c : c + 128], add_noise)
            hb[...] = half[...].astype(BF16)
            hr[...] = jnp.concatenate([half[i * COLS : i * COLS + 8, :] for i in range(ROWS)], axis=0).astype(BF16)
            early = [
                pltpu.make_async_remote_copy(
                    src, dst, send_sem.at[32 + n], recv_sem.at[32 + n], device_id=who, device_id_type=MESH
                )
                for n, (src, dst, who) in enumerate(
                    [
                        (hb.at[pl.ds(0, 256)], hn_below, (above, tx)),
                        (hr, hn_right, (ty, left)),
                        (hr.at[pl.ds(0, 64)], hn_corner, (above, left)),
                    ]
                )
            ]
            for copy in early:
                copy.start()
            for i in range(ROWS):
                hpad[i, 0:COLS, :] = half[i * COLS : i * COLS + COLS, :]

        def bias1(n):
            wi, wk = n // 4, n % 4

            def label(x):
                return 3 * region(ty * ROWS + wi * 8 + x // 8, sr) + region(tx * COLS + wk * 8 + x % 8, sc_)

            return jnp.where(label(key) == label(query), 0.0, -1e30)

        def shifted(start, count):
            swin_rows(flow, qkv, att, start, count, bias1, w_qkv, w_proj, w_up, w_down, norm_gains, 1)
            rows = slice(start * 64, (start + count) * 64)
            est = mm(flow[rows, :].astype(BF16), w_unembed[...])
            eb[start : start + count] = est.astype(BF16).reshape(count, 64, PIX)
            return est

        def place(est, start, count):
            for n in range(start, start + count):
                wi, wk = n // 4, n % 4
                for p in range(8):
                    row = (n - start) * 64 + p * 8
                    around[8 + wi * 8 + p, 8 + wk * 8 : 16 + wk * 8, :] = est[row : row + 8, :]

        for p in range(8):
            rolled = pltpu.roll(padded[p + sr, 0:COLS, :], COLS - sc_, 0)
            for wk in range(3):
                row = wk * 64 + p * 8
                flow[row : row + 8, :] = rolled[wk * 8 : wk * 8 + 8, :]
        place(shifted(0, 3), 0, 3)
        for copy in sends:
            copy.wait()
        sends.clear()
        for p in range(8):
            for wk in range(4):
                padded[16 + p, wk * 8 : wk * 8 + 8, :] = from_below[t, wk, p * 8 : p * 8 + 8, :].astype(F32)
            for wi in range(2):
                at = wi * 64 + p * 8
                padded[wi * 8 + p, 32:40, :] = from_right[t, at : at + 8, :].astype(F32)
            padded[16 + p, 32:40, :] = from_corner[t, p * 8 : p * 8 + 8, :].astype(F32)
        for i in range(ROWS):
            rolled = pltpu.roll(padded[i + sr], COLS + 8 - sc_, 0)
            for wk in range(3 if i < 8 else 0, 4):
                row = ((i // 8 * 4 + wk) * 8 + i % 8) * 8
                flow[row : row + 8, :] = rolled[wk * 8 : wk * 8 + 8, :]
        est = shifted(3, 5)
        back = []
        for n, (src, dst, who) in enumerate(
            [
                (eb.at[pl.ds(4, 4)], to_below.at[t], (below, tx)),
                (eb.at[3], to_right.at[t, 0], (ty, right)),
                (eb.at[7], to_right.at[t, 1], (ty, right)),
                (eb.at[7], to_corner.at[t], (below, right)),
            ]
        ):
            copy = pltpu.make_async_remote_copy(
                src, dst, send_sem.at[base + 11 + n], recv_sem.at[base + 11 + n], device_id=who, device_id_type=MESH
            )
            copy.start()
            back.append(copy)
        returning.append(back)
        place(est, 3, 5)
        if t + 1 < STEPS:
            for copy in early:
                copy.wait()
            for p in range(8):
                hpad[16 + p, 0:COLS, :] = hn_below[p * COLS : p * COLS + COLS, :].astype(F32)
                hpad[16 + p, COLS : COLS + 8, :] = hn_corner[p * 8 : p * 8 + 8, :].astype(F32)
            for i in range(ROWS):
                hpad[i, COLS : COLS + 8, :] = hn_right[i * 8 : i * 8 + 8, :].astype(F32)
            for i in range(ROWS):
                ahead = pltpu.roll(hpad[i + sr], COLS + 8 - sc_, 0)[:COLS]
                ahead = ahead - SIGMAS[t] * around[8 + i, 8 : 8 + COLS, :]
                sa[i // 2, i % 2 * COLS : i % 2 * COLS + COLS, :] = ahead.astype(BF16)
        else:
            roll_back(t)

            def give(row, lane, piece):
                out[row : row + 8, lane : lane + 128] = piece

            patches_to_pixels(lambda r, c: state[r : r + 8, c : c + 128], give)


def per_device(consts, image, noise, offsets, key_mask, gains, observed, vis_weight, w_embed, w_qkv, w_proj, w_up, w_down, w_unembed, norm_gains):
    w1, w4, tw1, f1, f2, w2, w3, tw2, tw3, m2, m3, ph = consts
    arrays = dict(
        image=image, key_mask=key_mask, w1=w1, tw1=tw1, f1=f1, gains=gains, observed=observed, weight=vis_weight,
        w2=w2, w3=w3, tw2=tw2, tw3=tw3, m2=m2, m3=m3, f2=f2, w4=w4, ph=ph, norm_gains=norm_gains, w_embed=w_embed,
        w_qkv=w_qkv, w_proj=w_proj, w_up=w_up, w_down=w_down, w_unembed=w_unembed, noise=noise,
    )
    moved = [arrays[name] for name in NAMES]
    V = pltpu.VMEM
    held = [V(x.shape[1:] if name == "noise" else x.shape, x.dtype) for name, x in zip(NAMES, moved)]
    scratch = held + [
        V((TOKENS, PIX), F32),
        V((TOKENS, PIX), F32),
        V((NTX, 64, PIX), BF16),
        V((STEPS, NTX, 64, PIX), BF16),
        V((DEV, 16, 128), BF16),
        V((STEPS, DEV, 16, 128), BF16),
        V((DEV, 16, 128), BF16),
        V((STEPS, DEV, 16, 128), BF16),
        V((2, NTX, 32, PIX), BF16),
        V((STEPS, 2, NTX, 32, PIX), BF16),
        V((DEV * 16, 128), F32),
        V((1024, 128), F32),
        V((3, 64, 2048), F32),
        V((TOKENS, D), F32),
        V((TOKENS, 3 * D), BF16),
        V((TOKENS, D), BF16),
        V((TOKENS, D), BF16),
        V((ROWS + 8, COLS + 8, D), F32),
        V((ROWS + 8, COLS + 8, PIX), F32),
        V((STEPS, 128, D), BF16),
        V((STEPS, 4, 64, D), BF16),
        V((STEPS, 64, D), BF16),
        V((STEPS, 2, 64, PIX), BF16),
        V((STEPS, 4, 64, PIX), BF16),
        V((STEPS, 64, PIX), BF16),
        V((8, 128, 64), F32),
        V((2048, 256), BF16),
        V((8, 64, PIX), BF16),
        V((TOKENS, PIX), BF16),
        V((128, PIX), BF16),
        V((ROWS + 8, COLS + 8, PIX), F32),
        V((256, PIX), BF16),
        V((128, PIX), BF16),
        V((64, PIX), BF16),
        pltpu.SemaphoreType.DMA((len(NAMES),)),
        pltpu.SemaphoreType.DMA((STEPS * 16 + 3,)),
        pltpu.SemaphoreType.DMA((STEPS * 16 + 3,)),
        pltpu.SemaphoreType.DMA((STEPS * 2 * 4,)),
        pltpu.SemaphoreType.REGULAR,
    ]
    stepped = pl.pallas_call(
        kernel,
        out_shape=jax.ShapeDtypeStruct(image.shape, F32),
        in_specs=[pl.BlockSpec(memory_space=pltpu.SMEM)] + [pl.BlockSpec(memory_space=pl.ANY)] * len(NAMES),
        out_specs=pl.BlockSpec(memory_space=pltpu.VMEM),
        scratch_shapes=scratch,
        compiler_params=pltpu.CompilerParams(collective_id=0, has_side_effects=True, vmem_limit_bytes=60 * 2**20),
    )(offsets, *moved)
    return stepped + SIGMAS[STEPS] * noise[STEPS - 1]


def solution(mesh):
    consts = tables()
    in_specs = (
        P("ty", "tx"),
        P(None, "ty", "tx"),
        P(),
        P("ty", "tx"),
        P(None, ("ty", "tx"), None),
        P(None, ("ty", "tx"), None),
        P(("ty", "tx"), None),
        P(),
        P(),
        P(),
        P(),
        P(),
        P(),
        P(),
    )
    consts_specs = (P(),) * len(consts)
    mapped = jax.shard_map(
        lambda c, *args: per_device(c, *args),
        mesh=mesh,
        in_specs=(consts_specs,) + in_specs,
        out_specs=P("ty", "tx"),
        check_vma=False,
    )
    return lambda *args: mapped(tuple(jnp.asarray(c) for c in consts), *args)
```
